256 devices in a mesh: seq: 32 (over y, z), head: 8 (over x, core).
Axes of the slice: x: 4, y: 4, z: 8, core: 2. Of those that a mesh axis runs over, the one named last changes fastest.
Arguments:
- vertex_features: bfloat16 [262144, 512], P(('seq', 'head')), may hold values from -48 to 48
- entry_rescaling_gain: float32 [512], replicated, may hold values from 0.1 to 1.9
- sharpness_factor: float32 [8], replicated, may hold values from 4 to 20
- triple_projection_matrix: bfloat16 [512, 3, 512], P(None, None, 'head'), may hold values from -0.25 to 0.25
- final_projection_matrix: bfloat16 [512, 512], replicated, may hold values from -0.25 to 0.25
- occupied_tile_targets: int32 [2048, 12], P('seq'), may hold values from 0 to 2047, as said below
Outputs:
- mixed: bfloat16 [262144, 512], P(('seq', 'head'))
The draws below stay inside these ranges and needn't reach their ends.
Inputs may be any that keep to these rules, and one draw needn't show every extreme that they name: `occupied_tile_targets`: each block row lists 12 different column blocks, among them its own block, and exactly 10 of them lie in its own group (block rows g * 64 to g * 64 + 63 form group g). The block rows of one group together list at most 6 entries that lie in any one other group.
All inputs are finite; a program needn't handle non-finite values.
Results may differ from the reference program's by a relative error of at most 0.0091.
Values may be sent and summed in bfloat16 or wider, within the bound.
A program may use at most 64 MiB of HBM per device.

```python
import math
import jax
import jax.numpy as jnp
from jax import lax

D = 512
ATTN_UNIT_COUNT = 8
ATTN_UNIT_WIDTH = 64
BLK = 128
KB = 12
KL = 10
BR_DEV = 64
NB = 2048
NODES = 262144
CAP = 6
N_SEQ = 32


def draw_vertex_features(key, part):
    key = jax.random.fold_in(key, 5)
    key_value, key_row, key_column = jax.random.split(key, 3)
    base = jnp.clip(jax.random.normal(key_value, (NODES, D), jnp.float32), -4.0, 4.0)
    row_low = 0.25
    row_high = 4.0
    row_scale = jnp.exp(jax.random.uniform(key_row, (NODES, 1), jnp.float32, math.log(row_low), math.log(row_high)))
    column_scale = jnp.exp(jax.random.uniform(key_column, (1, D), jnp.float32, math.log(0.3), math.log(3.0)))
    return (base * row_scale * column_scale).astype(jnp.bfloat16)


def draw_occupied_tile_targets(key, part):
    key = jax.random.fold_in(key, 9)
    key_local, key_owner, key_hot, key_pick, key_order = jax.random.split(key, 5)
    far_width = KB - KL
    remote = BR_DEV * far_width
    row_ids = jnp.arange(NB, dtype=jnp.int32)
    owner_group = row_ids // BR_DEV
    within = row_ids % BR_DEV

    def near_offsets(subkey):
        return jax.random.permutation(subkey, BR_DEV - 1)[:KL - 1].astype(jnp.int32) + 1
    offsets = jax.vmap(near_offsets)(jax.random.split(key_local, NB))
    near_list = jnp.concatenate([jnp.zeros((NB, 1), jnp.int32), offsets], axis=1)
    near_columns = owner_group[:, None] * BR_DEV + (within[:, None] + near_list) % BR_DEV

    def owner_offsets(subkey):
        key_first, key_second, key_third = jax.random.split(subkey, 3)
        owner_order = jax.random.permutation(key_first, N_SEQ - 1).astype(jnp.int32) + 1
        full_slots = jnp.repeat(owner_order[:2], CAP)
        spare_slots = jnp.repeat(owner_order[2:], CAP)
        chosen = jax.random.permutation(key_second, spare_slots)[:remote - 2 * CAP]
        return jax.random.permutation(key_third, jnp.concatenate([full_slots, chosen]))
    far_offsets = jax.vmap(owner_offsets)(jax.random.split(key_owner, N_SEQ))
    far_owner = ((jnp.arange(N_SEQ, dtype=jnp.int32)[:, None] + far_offsets) % N_SEQ).reshape(NB, far_width)
    hot_order = jax.vmap(lambda subkey: jax.random.permutation(subkey, BR_DEV).astype(jnp.int32))(jax.random.split(key_hot, N_SEQ))
    uniform_draws = jax.random.randint(key_pick, (3, NB, N_SEQ), 0, BR_DEV, dtype=jnp.int32)
    lowest = jnp.min(uniform_draws, axis=0)
    same_owner = far_owner[:, :, None] == far_owner[:, None, :]
    earlier = jnp.arange(far_width)[None, :] < jnp.arange(far_width)[:, None]
    slot_rank = jnp.sum(jnp.logical_and(same_owner, earlier[None]), axis=2).astype(jnp.int32)
    start_pos = jnp.take_along_axis(lowest, far_owner, axis=1)
    position = (start_pos + slot_rank) % BR_DEV
    far_columns = far_owner * BR_DEV + hot_order[far_owner, position]
    columns = jnp.concatenate([near_columns, far_columns], axis=1)
    shuffle = jax.vmap(lambda subkey: jax.random.permutation(subkey, KB).astype(jnp.int32))(jax.random.split(key_order, NB))
    return jnp.take_along_axis(columns, shuffle, axis=1).astype(jnp.int32)


def level_of(key, dims, cuts, low, largest):
    factor_of, own = 1.0, jax.random.fold_in(key, 6)
    for dim, shards_of in cuts:
        draws = jnp.exp(jax.random.uniform(jax.random.fold_in(own, dim), (shards_of,), jnp.float32, low / len(cuts), largest / len(cuts)))
        factor_of = factor_of * jnp.repeat(draws, dims[dim] // shards_of).reshape([-1 if axis == dim else 1 for axis in range(len(dims))])
    return factor_of


def bell_draw(stream_key, shape, width, reach, pieces=(), kind=jnp.bfloat16):
    loudness = level_of(stream_key, shape, pieces, -0.22, 0.18) if pieces else 1.0
    result = jax.random.normal(stream_key, shape, jnp.float32) * width * loudness
    return jnp.minimum(jnp.maximum(result, -reach), reach).astype(kind)


def setup_inputs(seed: int = 0) -> dict:
    key_of = jax.random.split(jax.random.key(seed), 7)
    vertex_features = draw_vertex_features(jax.random.fold_in(key_of[6], 71), 0)
    entry_rescaling_gain = jnp.clip(1.0 + 0.18 * jax.random.normal(key_of[1], (D,), jnp.float32), 0.1, 1.9)
    sharpness_factor = jnp.clip(jnp.exp(jax.random.uniform(key_of[2], (ATTN_UNIT_COUNT,), jnp.float32, math.log(4.0), math.log(20.0))), 4.0, 20.0)
    triple_projection_matrix = bell_draw(key_of[3], (D, 3, D), D ** -0.5, 0.25, ((2, 8),))
    final_projection_matrix = bell_draw(key_of[4], (D, D), D ** -0.5, 0.25)
    occupied_tile_targets = draw_occupied_tile_targets(jax.random.fold_in(key_of[6], 71), 0)
    return dict(vertex_features=vertex_features, entry_rescaling_gain=entry_rescaling_gain, sharpness_factor=sharpness_factor, triple_projection_matrix=triple_projection_matrix, final_projection_matrix=final_projection_matrix, occupied_tile_targets=occupied_tile_targets)


def rms_rows(values, epsilon):
    return values * lax.rsqrt(lax.optimization_barrier(jnp.mean(values * values, axis=-1, keepdims=True)) + epsilon)

def rounded(values):
    return lax.optimization_barrier(values.astype(jnp.bfloat16))

def reference(vertex_features, entry_rescaling_gain, sharpness_factor, triple_projection_matrix, final_projection_matrix, occupied_tile_targets):
    normed = (rms_rows(vertex_features.astype(jnp.float32), 1e-06) * entry_rescaling_gain).astype(jnp.bfloat16)
    projected = jnp.dot(normed, triple_projection_matrix.reshape(D, 3 * D), preferred_element_type=jnp.float32)
    projected = rounded(projected).reshape(NODES, 3, ATTN_UNIT_COUNT, ATTN_UNIT_WIDTH)
    queries = rounded(rms_rows(projected[:, 0].astype(jnp.float32), 1e-06))
    key_rows = rounded(rms_rows(projected[:, 1].astype(jnp.float32), 1e-06))
    value_rows = projected[:, 2]
    key_blocks = key_rows.reshape(NB, BLK, ATTN_UNIT_COUNT, ATTN_UNIT_WIDTH)
    value_blocks = value_rows.reshape(NB, BLK, ATTN_UNIT_COUNT, ATTN_UNIT_WIDTH)
    query_blocks = queries.reshape(NB, BLK, ATTN_UNIT_COUNT, ATTN_UNIT_WIDTH)
    sharpened_similarity = (sharpness_factor / ATTN_UNIT_WIDTH)[:, None, None]
    centered_similarity = sharpness_factor[:, None, None]

    def one_row(inputs):
        query_block, column_list = inputs
        listed_keys = key_blocks[column_list].reshape(KB * BLK, ATTN_UNIT_COUNT, ATTN_UNIT_WIDTH).astype(jnp.float32)
        listed_values = value_blocks[column_list].reshape(KB * BLK, ATTN_UNIT_COUNT, ATTN_UNIT_WIDTH).astype(jnp.float32)
        scores = jnp.einsum('qhd,khd->hqk', query_block.astype(jnp.float32), listed_keys) * sharpened_similarity
        weights = jnp.exp(scores - centered_similarity)
        totals = lax.optimization_barrier(jnp.sum(weights, axis=-1))
        chances = rounded(weights).astype(jnp.float32)
        mixture = jnp.einsum('hqk,khd->qhd', chances, listed_values) / jnp.transpose(totals)[:, :, None]
        return mixture.astype(jnp.bfloat16)
    attended = lax.map(one_row, (query_blocks, occupied_tile_targets)).reshape(NODES, D)
    return jnp.dot(attended, final_projection_matrix, preferred_element_type=jnp.float32).astype(jnp.bfloat16)
```

```python
import math
import jax
import jax.numpy as jnp
from jax import lax
from jax.experimental import pallas as pl
from jax.experimental.pallas import tpu as pltpu
from jax.sharding import PartitionSpec as P

MESH = pl.DeviceIdType.MESH
BF = jnp.bfloat16
F32 = jnp.float32
GROUPS = 32
PARTS = 8
HEADS = 8
WIDTH = 64
BLK = 128
KL = 10
FAR = 2
CAP = 6
ROWS = 8
GROUP_BLOCKS = 64
SUB = 16
CHUNKS = 4
LANES = 128
LOG2E = math.log2(math.e)
EPS = 1e-06


def wait_bytes(ref, sem):
    pltpu.make_async_copy(ref, ref, sem).wait()


def kernel(
    x_ref, gain_ref, w_ref, wf_ref, req_ref, sharp_ref, pos_ref, loc_ref,
    out_ref,
    x_all, w_all, kv, kvr, q_all, acc, xa0, xa1, xa2, xa3, zr0, zr1, zr2, zr3,
    zs, xs, xr, rq, rqs, att,
    xa_ss, xa_rs, rq_ss, rq_rs, rq_ls, w_ss, w_rs, ag_ss, ag_rs, z_ss, z_rs, xr_ss, xr_rs,
):
    me = lax.axis_index("seq")
    mh = lax.axis_index("head")
    core = lax.rem(mh, 2)
    right = lax.rem(mh + 2, PARTS)
    left = lax.rem(mh + 6, PARTS)
    opp = lax.rem(mh + 4, PARTS)
    sib = mh + 1 - 2 * core
    sib_right = right + 1 - 2 * core
    sib_left = left + 1 - 2 * core
    sib_opp = opp + 1 - 2 * core
    xas = (xa0, xa1, xa2, xa3)
    zrs = (zr0, zr1, zr2, zr3)

    barrier = pltpu.get_barrier_semaphore()

    def greet_seq(d, carry):
        pl.semaphore_signal(barrier, inc=1, device_id={"seq": lax.rem(me + d, GROUPS)}, device_id_type=MESH)
        return carry

    def greet_head(d, carry):
        pl.semaphore_signal(barrier, inc=1, device_id={"head": lax.rem(mh + d, PARTS)}, device_id_type=MESH)
        return carry

    lax.fori_loop(1, GROUPS, greet_seq, 0)
    lax.fori_loop(1, PARTS, greet_head, 0)

    gain = gain_ref[...]

    def norm_block(i, carry):
        rows = x_ref[pl.ds(pl.multiple_of(i * BLK, BLK), BLK), :].astype(F32)
        scale = lax.rsqrt(jnp.mean(rows * rows, axis=-1, keepdims=True) + EPS)
        x_all[mh, i] = (rows * scale * gain).astype(BF)
        return carry

    lax.fori_loop(0, ROWS, norm_block, 0)
    w_all[mh] = w_ref[...]
    rq[me] = req_ref[me]

    pl.semaphore_wait(barrier, GROUPS - 1 + PARTS - 1)

    def send_sub(c):
        def go(d, carry):
            t = lax.rem(mh + d, PARTS)
            pltpu.make_async_remote_copy(
                src_ref=x_all.at[mh, :, pl.ds(pl.multiple_of(t * SUB, SUB), SUB), pl.ds(c * LANES, LANES)],
                dst_ref=xas[c].at[pl.ds(mh * ROWS, ROWS)],
                send_sem=xa_ss.at[c], recv_sem=xa_rs.at[c],
                device_id={"head": t}, device_id_type=MESH,
            ).start()
            return carry

        lax.fori_loop(1, PARTS, go, 0)
        xas[c][pl.ds(mh * ROWS, ROWS)] = x_all[
            mh, :, pl.ds(pl.multiple_of(mh * SUB, SUB), SUB), pl.ds(c * LANES, LANES)]

    def send_req(d, carry):
        t = lax.rem(me + d, GROUPS)
        pltpu.make_async_remote_copy(
            src_ref=req_ref.at[t], dst_ref=rq.at[me], send_sem=rq_ss, recv_sem=rq_rs,
            device_id={"seq": t}, device_id_type=MESH,
        ).start()
        return carry

    def ring(buf, ss, rs, half):
        first, second = pl.ds(0, half), pl.ds(half, half)

        def copy(k, view, to):
            return pltpu.make_async_remote_copy(
                src_ref=view, dst_ref=view, send_sem=ss.at[k], recv_sem=rs.at[k],
                device_id={"head": to}, device_id_type=MESH)

        return (
            copy(0, buf.at[mh], right), copy(1, buf.at[mh], left), copy(2, buf.at[mh], sib),
            copy(3, buf.at[left, first], right), copy(4, buf.at[right, second], left),
            copy(5, buf.at[left], sib), copy(6, buf.at[right], sib), copy(7, buf.at[opp], sib),
        )

    w_ring = ring(w_all, w_ss, w_rs, w_all.shape[1] // 2)
    x_ring = ring(x_all, ag_ss, ag_rs, ROWS // 2)

    send_sub(0)
    lax.fori_loop(1, GROUPS, send_req, 0)
    for k in (0, 1, 2):
        w_ring[k].start()
    for c in range(1, CHUNKS):
        send_sub(c)
    for k in (0, 1, 2):
        x_ring[k].start()

    wait_bytes(rq.at[pl.ds(0, GROUPS - 1)], rq_rs)
    to_smem = pltpu.make_async_copy(rq, rqs, rq_ls)
    to_smem.start()
    to_smem.wait()

    def send_groups(c):
        wait_bytes(xas[c].at[pl.ds(0, GROUP_BLOCKS - ROWS)], xa_rs.at[c])

        def go(d, carry):
            t = lax.rem(me + d, GROUPS)
            for s in range(CAP):
                zs[c, t * CAP + s] = xas[c][rqs[t, 0, s]]
            pltpu.make_async_remote_copy(
                src_ref=zs.at[c, pl.ds(t * CAP, CAP)], dst_ref=zrs[c].at[pl.ds(me * CAP, CAP)],
                send_sem=z_ss.at[c], recv_sem=z_rs.at[c],
                device_id={"seq": t}, device_id_type=MESH,
            ).start()
            return carry

        lax.fori_loop(1, GROUPS, go, 0)

    send_groups(0)
    w_ring[0].wait_recv()
    w_ring[1].wait_recv()
    for k in (3, 4, 5, 6):
        w_ring[k].start()
    send_groups(1)
    w_ring[3].wait_recv()
    w_ring[4].wait_recv()
    w_ring[7].start()
    send_groups(2)
    send_groups(3)
    for k in (2, 5, 6, 7):
        w_ring[k].wait_recv()

    lane2 = lax.broadcasted_iota(jnp.int32, (1, 2 * LANES), 1)
    is_key = lax.rem(lane2, LANES) < WIDTH
    row2 = lax.broadcasted_iota(jnp.int32, (2 * LANES, 2 * LANES), 0)
    col2 = lax.broadcasted_iota(jnp.int32, (2 * LANES, 2 * LANES), 1)
    same = jnp.logical_and(row2 // LANES == col2 // LANES, lax.rem(row2, LANES) < WIDTH)
    spread = jnp.where(same, 1.0 / WIDTH, 0.0).astype(BF)
    lane1 = lax.broadcasted_iota(jnp.int32, (1, LANES), 1)
    low = lane1 < WIDTH

    def unit_rows(rounded):
        wide = rounded.astype(F32)
        mean = jnp.dot((wide * wide).astype(BF), spread, preferred_element_type=F32)
        return wide, wide * lax.rsqrt(mean + EPS)

    def keys_values(rows, p):
        pair = jnp.concatenate([w_all[2 * p, 0:512, :], w_all[2 * p + 1, 0:512, :]], axis=1)
        rounded = jnp.dot(rows, pair, preferred_element_type=F32).astype(BF)
        wide, unit = unit_rows(rounded)
        return jnp.where(is_key, unit, wide).astype(BF)

    def project(s):
        def go(i, carry):
            rows = x_all[s, pl.ds(2 * i, 2)].reshape(2 * BLK, 512)
            for p in range(HEADS // 2):
                both = keys_values(rows, p)
                for n in range(2):
                    for m in range(2):
                        kv[s * ROWS + 2 * i + m, 2 * p + n] = both[m * BLK:(m + 1) * BLK, n * LANES:(n + 1) * LANES]
            return carry

        lax.fori_loop(0, ROWS // 2, go, 0)

    def project_queries():
        def go(b, carry):
            rows = x_all[mh, b]
            for p in range(HEADS // 2):
                pair = jnp.concatenate([w_all[2 * p, 512:768, :], w_all[2 * p + 1, 512:768, :]], axis=1)
                one = jnp.dot(rows[:, 0:256], pair, preferred_element_type=F32)
                two = jnp.dot(rows[:, 256:512], pair, preferred_element_type=F32)
                two = jnp.concatenate(
                    [pltpu.roll(two[:, 0:LANES], WIDTH, 1), pltpu.roll(two[:, LANES:2 * LANES], WIDTH, 1)], axis=1)
                unused, unit = unit_rows((one + two).astype(BF))
                unit = jnp.where(is_key, unit, 0.0).astype(BF)
                q_all[b, 2 * p] = unit[:, 0:LANES]
                q_all[b, 2 * p + 1] = unit[:, LANES:2 * LANES]
            return carry

        lax.fori_loop(0, ROWS, go, 0)

    def attend(q, pair, scale, shift):
        scores = lax.dot_general(q, pair, (((1,), (1,)), ((), ())), preferred_element_type=F32)
        weights = jnp.exp2(scores * scale - shift).astype(BF)
        counted = jnp.where(low, jnp.ones_like(pair), pair)
        return jnp.dot(weights, counted, preferred_element_type=F32)

    def near(first, last):
        def go(u, carry):
            b, h = u // HEADS, lax.rem(u, HEADS)
            q = q_all[b, h]
            sharp = sharp_ref[h]
            scale, shift = sharp * (LOG2E / WIDTH), sharp * LOG2E
            base = (mh * ROWS + b) * KL
            total = jnp.zeros((BLK, LANES), F32)
            for j in range(KL // 2):
                pair = jnp.concatenate([kv[loc_ref[base + 2 * j], h], kv[loc_ref[base + 2 * j + 1], h]], axis=0)
                total = total + attend(q, pair, scale, shift)
            acc[b, h] = total
            return carry

        lax.fori_loop(first, last, go, 0)

    def pass_on(c):
        wait_bytes(zrs[c].at[pl.ds(0, (GROUPS - 1) * CAP)], z_rs.at[c])

        def go(d, carry):
            t = lax.rem(mh + d, PARTS)
            for e in range(ROWS * FAR):
                xs[c, t, e] = zrs[c][pos_ref[t * (ROWS * FAR) + e]]

            @pl.when(d < PARTS)
            def _():
                pltpu.make_async_remote_copy(
                    src_ref=xs.at[c, t], dst_ref=xr.at[mh, :, :, pl.ds(c * LANES, LANES)],
                    send_sem=xr_ss.at[c], recv_sem=xr_rs.at[c],
                    device_id={"head": t}, device_id_type=MESH,
                ).start()

            return carry

        lax.fori_loop(1, PARTS + 1, go, 0)
        xr[mh, :, :, pl.ds(c * LANES, LANES)] = xs[c, mh]

    project(mh)
    x_ring[0].wait_recv()
    x_ring[1].wait_recv()
    for k in (3, 4, 5, 6):
        x_ring[k].start()
    x_ring[2].wait_recv()
    project(sib)
    project(left)
    project(right)
    pass_on(0)
    x_ring[3].wait_recv()
    x_ring[4].wait_recv()
    x_ring[7].start()
    project(opp)
    x_ring[5].wait_recv()
    project(sib_left)
    x_ring[6].wait_recv()
    project(sib_right)
    pass_on(1)
    project_queries()
    x_ring[7].wait_recv()
    project(sib_opp)
    near(0, ROWS * HEADS // 2)
    pass_on(2)
    near(ROWS * HEADS // 2, ROWS * HEADS)
    pass_on(3)
    for c in range(CHUNKS):
        wait_bytes(xs.at[c, pl.ds(0, PARTS - 1)], xr_rs.at[c])

    def project_far(s, carry):
        rows = xr[s].reshape(ROWS * FAR * SUB, 512)
        for p in range(HEADS // 2):
            both = keys_values(rows, p)
            for n in range(2):
                kvr[2 * p + n, :, pl.ds(pl.multiple_of(s * SUB, SUB), SUB), :] = both[
                    :, n * LANES:(n + 1) * LANES].reshape(ROWS * FAR, SUB, LANES)
        return carry

    lax.fori_loop(0, PARTS, project_far, 0)

    def finish(b, carry):
        for p in range(HEADS // 2):
            sums = []
            for h in (2 * p, 2 * p + 1):
                sharp = sharp_ref[h]
                pair = kvr[h, pl.ds(FAR * b, FAR)].reshape(FAR * BLK, LANES)
                sums.append(acc[b, h] + attend(q_all[b, h], pair, sharp * (LOG2E / WIDTH), sharp * LOG2E))
            even, odd = sums
            even_turned, odd_turned = pltpu.roll(even, WIDTH, 1), pltpu.roll(odd, WIDTH, 1)
            ratio = jnp.where(low, even_turned, odd) / jnp.where(low, even, odd_turned)
            att[:, p * LANES:(p + 1) * LANES] = ratio.astype(BF)
        out_ref[pl.ds(pl.multiple_of(b * BLK, BLK), BLK), :] = jnp.dot(
            att[...], wf_ref[...], preferred_element_type=F32).astype(BF)
        return carry

    lax.fori_loop(0, ROWS, finish, 0)

    wait_bytes(rq.at[pl.ds(0, GROUPS - 1)], rq_ss)
    for c in range(CHUNKS):
        wait_bytes(xas[c].at[pl.ds(0, GROUP_BLOCKS - ROWS)], xa_ss.at[c])
        wait_bytes(zs.at[c, pl.ds(0, (GROUPS - 1) * CAP)], z_ss.at[c])
        wait_bytes(xs.at[c, pl.ds(0, PARTS - 1)], xr_ss.at[c])
    for k in range(8):
        w_ring[k].wait_send()
        x_ring[k].wait_send()


def lists_of(targets, group):
    owner, within = targets // GROUP_BLOCKS, targets % GROUP_BLOCKS
    far = owner != group
    width = targets.shape[1]
    earlier = jnp.arange(width)[:, None] < jnp.arange(width)[None, :]

    def rank_of(flag):
        return jnp.sum(jnp.where(jnp.logical_and(flag[:, :, None], earlier[None]), 1, 0), axis=1)

    def picked(flag, rank, values, count):
        hit = jnp.logical_and(flag[:, :, None], rank[:, :, None] == jnp.arange(count)[None, None, :])
        return jnp.sum(jnp.where(hit, values[:, :, None], 0), axis=1)

    near = jnp.logical_not(far)
    loc = picked(near, rank_of(near), within, KL).reshape(-1)
    far_rank = rank_of(far)
    entry_owner = picked(far, far_rank, owner, FAR).reshape(-1)
    entry_within = picked(far, far_rank, within, FAR).reshape(-1)
    entries = jnp.arange(entry_owner.shape[0])
    same = entry_owner[:, None] == entry_owner[None, :]
    slot = jnp.sum(jnp.where(jnp.logical_and(same, entries[:, None] < entries[None, :]), 1, 0), axis=0)
    pos = entry_owner * CAP + slot
    asked = jnp.arange(GROUPS * LANES)
    code = entry_owner * LANES + slot
    req = jnp.sum(jnp.where(asked[:, None] == code[None, :], entry_within[None, :], 0), axis=1)
    return loc, pos, req.reshape(GROUPS, 1, LANES)


def on_device(x, gain, sharp, w3, wf, targets):
    loc, pos, req = lists_of(targets, lax.axis_index("seq"))
    w_kv = jnp.concatenate([w3[:, 1], w3[:, 2]], axis=1)
    w_q = jnp.concatenate([w3[0:256, 0], w3[256:512, 0]], axis=1)
    w_own = jnp.concatenate([w_kv, w_q], axis=0)
    vmem = pl.BlockSpec(memory_space=pltpu.VMEM)
    smem = pl.BlockSpec(memory_space=pltpu.SMEM)
    dma = pltpu.SemaphoreType.DMA
    sub = pltpu.VMEM((GROUP_BLOCKS, SUB, LANES), BF)
    landed = pltpu.VMEM((GROUPS * CAP, SUB, LANES), BF)
    return pl.pallas_call(
        kernel,
        out_shape=jax.ShapeDtypeStruct(x.shape, BF),
        in_specs=[vmem, vmem, vmem, vmem, vmem, smem, smem, smem],
        out_specs=vmem,
        scratch_shapes=[
            pltpu.VMEM((PARTS, ROWS, BLK, 512), BF),
            pltpu.VMEM((PARTS, 768, LANES), BF),
            pltpu.VMEM((GROUP_BLOCKS, HEADS, BLK, LANES), BF),
            pltpu.VMEM((HEADS, ROWS * FAR, BLK, LANES), BF),
            pltpu.VMEM((ROWS, HEADS, BLK, LANES), BF),
            pltpu.VMEM((ROWS, HEADS, BLK, LANES), F32),
            sub, sub, sub, sub, landed, landed, landed, landed,
            pltpu.VMEM((CHUNKS, GROUPS * CAP, SUB, LANES), BF),
            pltpu.VMEM((CHUNKS, PARTS, ROWS * FAR, SUB, LANES), BF),
            pltpu.VMEM((PARTS, ROWS * FAR, SUB, 512), BF),
            pltpu.VMEM((GROUPS, 1, LANES), jnp.int32),
            pltpu.SMEM((GROUPS, 1, LANES), jnp.int32),
            pltpu.VMEM((BLK, 512), BF),
            dma((CHUNKS,)), dma((CHUNKS,)), dma(()), dma(()), dma(()),
            dma((8,)), dma((8,)), dma((8,)), dma((8,)),
            dma((CHUNKS,)), dma((CHUNKS,)), dma((CHUNKS,)), dma((CHUNKS,)),
        ],
        compiler_params=pltpu.CompilerParams(
            collective_id=0, has_side_effects=True, vmem_limit_bytes=60 * 2**20),
        name="block_sparse_layer",
    )(x, gain.reshape(1, 512), w_own, wf, req, sharp, pos, loc)


def solution(mesh):
    placed = (P(("seq", "head"), None), P(), P(), P(None, None, "head"), P(), P("seq", None))
    return jax.shard_map(
        on_device, mesh=mesh, in_specs=placed, out_specs=P(("seq", "head"), None), check_vma=False
    )
```

```python
import math
import jax
import jax.numpy as jnp
from jax import lax
from jax.experimental import pallas as pl
from jax.experimental.pallas import tpu as pltpu
from jax.sharding import PartitionSpec as P

MESH = pl.DeviceIdType.MESH
BF = jnp.bfloat16
F32 = jnp.float32
GROUPS = 32
PARTS = 8
PAIRS = 4
WIDTH = 64
BLK = 128
KB = 12
KL = 10
FAR = 2
CAP = 6
RING = 8
ROWS = 8
GROUP_BLOCKS = 64
SUB = 16
CHUNKS = 4
LANES = 128
TOGETHER = 4
FINISH = 2
LOG2E = math.log2(math.e)
EPS = 1e-06


def wait_bytes(ref, sem):
    pltpu.make_async_copy(ref, ref, sem).wait()


def kernel(
    x_ref, gain_ref, w_ref, targets_ref, sharp_ref,
    out_ref,
    x_all, w_all, wk, wv, wq, kp, vp, kf, vf, q_all, num, den,
    xa0, xa1, xa2, xa3, zr0, zr1, zr2, zr3,
    zs, xs, xr, listing, req, rq, rqs, tab, tabs,
    xa_ss, xa_rs, rq_ss, rq_rs, rq_ls, tab_ls, w_ss, w_rs, ag_ss, ag_rs, z_ss, z_rs, xr_ss, xr_rs, far_rs,
):
    me = lax.axis_index("seq")
    mh = lax.axis_index("head")
    core = lax.rem(mh, 2)
    right = lax.rem(mh + 2, PARTS)
    left = lax.rem(mh + 6, PARTS)
    opp = lax.rem(mh + 4, PARTS)
    sib = mh + 1 - 2 * core
    sib_right = right + 1 - 2 * core
    sib_left = left + 1 - 2 * core
    sib_opp = opp + 1 - 2 * core
    xas = (xa0, xa1, xa2, xa3)
    zrs = (zr0, zr1, zr2, zr3)

    barrier = pltpu.get_barrier_semaphore()

    def greet_seq(d, carry):
        pl.semaphore_signal(barrier, inc=1, device_id={"seq": lax.rem(me + d, GROUPS)}, device_id_type=MESH)
        return carry

    def greet_head(d, carry):
        pl.semaphore_signal(barrier, inc=1, device_id={"head": lax.rem(mh + d, PARTS)}, device_id_type=MESH)
        return carry

    lax.fori_loop(1, GROUPS, greet_seq, 0)
    lax.fori_loop(1, PARTS, greet_head, 0)

    gain = gain_ref[...]

    def norm_block(i, carry):
        rows = x_ref[pl.ds(pl.multiple_of(i * BLK, BLK), BLK), :].astype(F32)
        scale = lax.rsqrt(jnp.mean(rows * rows, axis=-1, keepdims=True) + EPS)
        x_all[mh, i] = (rows * scale * gain).astype(BF)
        return carry

    lax.fori_loop(0, ROWS, norm_block, 0)

    pl.semaphore_wait(barrier, GROUPS - 1 + PARTS - 1)

    def send_sub(c):
        def go(d, carry):
            t = lax.rem(mh + d, PARTS)
            pltpu.make_async_remote_copy(
                src_ref=x_all.at[mh, :, pl.ds(pl.multiple_of(t * SUB, SUB), SUB), pl.ds(c * LANES, LANES)],
                dst_ref=xas[c].at[pl.ds(mh * ROWS, ROWS)],
                send_sem=xa_ss.at[c], recv_sem=xa_rs.at[c],
                device_id={"head": t}, device_id_type=MESH,
            ).start()
            return carry

        lax.fori_loop(1, PARTS, go, 0)
        xas[c][pl.ds(mh * ROWS, ROWS)] = x_all[
            mh, :, pl.ds(pl.multiple_of(mh * SUB, SUB), SUB), pl.ds(c * LANES, LANES)]

    send_sub(0)

    listing[...] = jnp.full(listing.shape, -GROUP_BLOCKS, jnp.int32)
    listing[0:KB, 0:GROUP_BLOCKS] = targets_ref[...]
    lane = lax.broadcasted_iota(jnp.int32, (1, LANES), 1)
    none = jnp.zeros((1, LANES), jnp.int32)
    near_count, far_count = none, none
    near_rows = [none] * KL
    owners, withins = [none] * FAR, [none] * FAR
    for j in range(KB):
        target = listing[j:j + 1, :]
        owner = lax.shift_right_arithmetic(target, 6)
        within = target - owner * GROUP_BLOCKS
        is_far = owner != me
        for k in range(KL):
            near_rows[k] = jnp.where(jnp.logical_and(owner == me, near_count == k), within, near_rows[k])
        for k in range(FAR):
            here = jnp.logical_and(is_far, far_count == k)
            owners[k] = jnp.where(here, owner, owners[k])
            withins[k] = jnp.where(here, within, withins[k])
        near_count = near_count + jnp.where(is_far, 0, 1)
        far_count = far_count + jnp.where(is_far, 1, 0)
    group = lax.broadcasted_iota(jnp.int32, (GROUPS, LANES), 0)
    hits = [jnp.where(group == owners[k], 1, 0) for k in range(FAR)]
    both = hits[0] + hits[1]
    counted = both
    wide_lane = lax.broadcasted_iota(jnp.int32, (GROUPS, LANES), 1)
    for step in (1, 2, 4, 8, 16, 32):
        counted = counted + jnp.where(wide_lane >= step, pltpu.roll(counted, step, 1), 0)
    counted = counted - both

    def over_groups(value):
        eight = value[0:8] + value[8:16] + value[16:24] + value[24:32]
        four = eight[0:4] + eight[4:8]
        two = four[0:2] + four[2:4]
        return two[0:1] + two[1:2]

    slots = [over_groups(hits[0] * counted), over_groups(hits[1] * (counted + hits[0]))]
    wanted = jnp.zeros((GROUPS, LANES), jnp.int32)
    for c in range(CAP):
        one = none
        for k in range(FAR):
            one = one + hits[k] * jnp.where(slots[k] == c, withins[k], 0)
        for step in (1, 2, 4, 8, 16, 32, 64):
            one = one + pltpu.roll(one, step, 1)
        wanted = jnp.where(wide_lane == c, one, wanted)
    for o in range(GROUPS):
        req[o] = wanted[o:o + 1, :]
    rq[me] = req[me]

    def send_req(d, carry):
        t = lax.rem(me + d, GROUPS)
        pltpu.make_async_remote_copy(
            src_ref=req.at[t], dst_ref=rq.at[me], send_sem=rq_ss, recv_sem=rq_rs,
            device_id={"seq": t}, device_id_type=MESH,
        ).start()
        return carry

    lax.fori_loop(1, GROUPS, send_req, 0)

    for k in range(KL):
        tab[k:k + 1, :] = near_rows[k]
    for k in range(FAR):
        tab[KL + k:KL + k + 1, :] = owners[k] * CAP + slots[k]
    tab[KB:16, :] = jnp.zeros((16 - KB, LANES), jnp.int32)
    to_tabs = pltpu.make_async_copy(tab, tabs, tab_ls)
    to_tabs.start()

    low = lane < WIDTH
    w_all[mh] = w_ref[...]

    def ring(buf, ss, rs, half):
        first, second = pl.ds(0, half), pl.ds(half, half)

        def copy(k, view, to):
            return pltpu.make_async_remote_copy(
                src_ref=view, dst_ref=view, send_sem=ss.at[k], recv_sem=rs.at[k],
                device_id={"head": to}, device_id_type=MESH)

        return (
            copy(0, buf.at[mh], right), copy(1, buf.at[mh], left), copy(2, buf.at[mh], sib),
            copy(3, buf.at[left, first], right), copy(4, buf.at[right, second], left),
            copy(5, buf.at[left], sib), copy(6, buf.at[right], sib), copy(7, buf.at[opp], sib),
        )

    w_ring = ring(w_all, w_ss, w_rs, w_all.shape[1] // 2)
    x_ring = ring(x_all, ag_ss, ag_rs, ROWS // 2)

    for k in (0, 1, 2):
        w_ring[k].start()
    for c in range(1, CHUNKS):
        send_sub(c)
    for k in (0, 1, 2):
        x_ring[k].start()

    wait_bytes(rq.at[pl.ds(0, GROUPS - 1)], rq_rs)
    to_smem = pltpu.make_async_copy(rq, rqs, rq_ls)
    to_smem.start()
    to_smem.wait()

    def send_groups(c):
        wait_bytes(xas[c].at[pl.ds(0, GROUP_BLOCKS - ROWS)], xa_rs.at[c])

        def one(dy, dz):
            t = lax.rem(me // RING + dy, GROUPS // RING) * RING + lax.rem(me + dz, RING)
            for s in range(CAP):
                zs[c, t * CAP + s] = xas[c][rqs[t, 0, s]]
            pltpu.make_async_remote_copy(
                src_ref=zs.at[c, pl.ds(t * CAP, CAP)], dst_ref=zrs[c].at[pl.ds(me * CAP, CAP)],
                send_sem=z_ss.at[c], recv_sem=z_rs.at[c],
                device_id={"seq": t}, device_id_type=MESH,
            ).start()

        def go(i, carry):
            dz = jnp.where(i % 2 == 0, 1 + i // 2, RING - 1 - i // 2)
            for dy in (0, 1, 3, 2):
                one(dy, dz)
            return carry

        lax.fori_loop(0, RING - 1, go, 0)
        for dy in (1, 3, 2):
            one(dy, 0)

    send_groups(0)
    w_ring[0].wait_recv()
    w_ring[1].wait_recv()
    for k in (3, 4, 5, 6):
        w_ring[k].start()
    send_groups(1)
    w_ring[3].wait_recv()
    w_ring[4].wait_recv()
    w_ring[7].start()
    send_groups(2)
    send_groups(3)
    for k in (2, 5, 6, 7):
        w_ring[k].wait_recv()
    to_tabs.wait()

    for k, ref in enumerate((wq, wk, wv)):
        for t in range(2):
            ref[t] = jnp.transpose(
                jnp.concatenate([w_all[4 * t + n, k * WIDTH:(k + 1) * WIDTH] for n in range(4)], axis=0), (1, 0))

    row2 = lax.broadcasted_iota(jnp.int32, (2 * LANES, 2 * LANES), 0)
    col2 = lax.broadcasted_iota(jnp.int32, (2 * LANES, 2 * LANES), 1)
    spread = jnp.where(row2 // WIDTH == col2 // WIDTH, 1.0 / WIDTH, 0.0).astype(BF)

    def unit_rows(rows, weights):
        wide = jnp.dot(rows, weights, preferred_element_type=F32).astype(BF).astype(F32)
        mean = jnp.dot((wide * wide).astype(BF), spread, preferred_element_type=F32)
        return (wide * lax.rsqrt(mean + EPS)).astype(BF)

    def plain_rows(rows, weights):
        return jnp.dot(rows, weights, preferred_element_type=F32).astype(BF)

    def project(s):
        def go(i, carry):
            rows = x_all[s, pl.ds(TOGETHER * i, TOGETHER)].reshape(TOGETHER * BLK, 512)
            for t in range(2):
                for ref, both in ((kp, unit_rows(rows, wk[t])), (vp, plain_rows(rows, wv[t]))):
                    for n in range(2):
                        for m in range(TOGETHER):
                            ref[s * ROWS + TOGETHER * i + m, 2 * t + n] = both[
                                m * BLK:(m + 1) * BLK, n * LANES:(n + 1) * LANES]
            return carry

        lax.fori_loop(0, ROWS // TOGETHER, go, 0)

    def project_queries():
        def go(i, carry):
            rows = x_all[mh, pl.ds(TOGETHER * i, TOGETHER)].reshape(TOGETHER * BLK, 512)
            for t in range(2):
                both = unit_rows(rows, wq[t])
                for n in range(2):
                    for m in range(TOGETHER):
                        one = both[m * BLK:(m + 1) * BLK, n * LANES:(n + 1) * LANES]
                        none = jnp.zeros_like(one)
                        q_all[TOGETHER * i + m, 2 * t + n, 0:BLK] = jnp.where(low, one, none)
                        q_all[TOGETHER * i + m, 2 * t + n, BLK:2 * BLK] = jnp.where(low, none, one)
            return carry

        lax.fori_loop(0, ROWS // TOGETHER, go, 0)

    def score(q, keys):
        return lax.dot_general(q, keys, (((1,), (1,)), ((), ())), preferred_element_type=F32)

    def blend(scores, values, p):
        weights = []
        for n in range(2):
            sharp = sharp_ref[2 * p + n]
            weights.append(jnp.exp2(
                scores[n * BLK:(n + 1) * BLK] * (sharp * (LOG2E / WIDTH)) - sharp * LOG2E).astype(BF))
        values = jnp.concatenate([values, jnp.ones_like(values)], axis=1)
        return jnp.dot(jnp.concatenate(weights, axis=0), values, preferred_element_type=F32)

    def parted(both):
        return (jnp.where(low, both[0:BLK, 0:LANES], both[BLK:2 * BLK, 0:LANES]),
                jnp.where(low, both[0:BLK, LANES:2 * LANES], both[BLK:2 * BLK, LANES:2 * LANES]))

    def near(first, last):
        def go(b, carry):
            listed = [tabs[j, mh * ROWS + b] for j in range(KL)]
            scores = [
                score(q_all[b, p], jnp.concatenate([kp[i, p] for i in listed], axis=0)) for p in range(PAIRS)]
            for p in range(PAIRS):
                both = blend(scores[p], jnp.concatenate([vp[i, p] for i in listed], axis=0), p)
                num[b, p], den[b, p] = parted(both)
            return carry

        lax.fori_loop(first, last, go, 0)

    def pass_on(c):
        wait_bytes(zrs[c].at[pl.ds(0, (GROUPS - 1) * CAP)], z_rs.at[c])

        def go(i, carry):
            t = lax.rem(mh + jnp.where(i % 2 == 0, 4 + i // 2, 3 - i // 2), PARTS)
            for e in range(ROWS * FAR):
                xs[c, t, e] = zrs[c][tabs[KL + e % FAR, t * ROWS + e // FAR]]

            @pl.when(i < PARTS - 1)
            def _():
                pltpu.make_async_remote_copy(
                    src_ref=xs.at[c, t], dst_ref=xr.at[mh, :, :, pl.ds(c * LANES, LANES)],
                    send_sem=xr_ss.at[c], recv_sem=xr_rs.at[c] if c < CHUNKS - 1 else far_rs.at[mh],
                    device_id={"head": t}, device_id_type=MESH,
                ).start()

            return carry

        lax.fori_loop(0, PARTS, go, 0)
        xr[mh, :, :, pl.ds(c * LANES, LANES)] = xs[c, mh]

    project(mh)
    x_ring[0].wait_recv()
    x_ring[1].wait_recv()
    for k in (3, 4, 5, 6):
        x_ring[k].start()
    x_ring[2].wait_recv()
    project(sib)
    project_queries()
    project(left)
    project(right)
    pass_on(0)
    x_ring[3].wait_recv()
    x_ring[4].wait_recv()
    x_ring[7].start()
    project(opp)
    x_ring[5].wait_recv()
    project(sib_left)
    x_ring[6].wait_recv()
    project(sib_right)
    pass_on(1)
    x_ring[7].wait_recv()
    project(sib_opp)
    near(0, ROWS // 2)
    pass_on(2)
    near(ROWS // 2, ROWS)
    pass_on(3)
    for c in range(CHUNKS - 1):
        wait_bytes(xs.at[c, pl.ds(0, PARTS - 1)], xr_rs.at[c])

    sources = (mh, sib, left, right, sib_left, sib_right, opp, sib_opp)

    def project_far(k):
        count = ROWS * FAR * SUB
        for s in sources[k:k + 2]:
            if s is not mh:
                wait_bytes(xs.at[CHUNKS - 1, 0], far_rs.at[s])
        rows = jnp.concatenate([xr[s].reshape(count, 512) for s in sources[k:k + 2]], axis=0)
        for t in range(2):
            for ref, both in ((kf, unit_rows(rows, wk[t])), (vf, plain_rows(rows, wv[t]))):
                for n in range(2):
                    for m in range(2):
                        ref[2 * t + n, :, (k + m) * SUB:(k + m + 1) * SUB, :] = both[
                            m * count:(m + 1) * count, n * LANES:(n + 1) * LANES].reshape(ROWS * FAR, SUB, LANES)

    def far_keys(ref, b, p):
        return ref[p, pl.ds(FAR * b, FAR)].reshape(FAR * BLK, LANES)

    def finish(i, carry):
        units = [(FINISH * i + m, p) for m in range(FINISH) for p in range(PAIRS)]
        scores = [score(q_all[b, p], far_keys(kf, b, p)) for b, p in units]
        for (b, p), one in zip(units, scores):
            top, bottom = parted(blend(one, far_keys(vf, b, p), p))
            out_ref[pl.ds(pl.multiple_of(b * BLK, BLK), BLK), p * LANES:(p + 1) * LANES] = (
                (num[b, p] + top) / (den[b, p] + bottom)).astype(BF)
        return carry

    for k in range(0, PARTS, 2):
        project_far(k)
    lax.fori_loop(0, ROWS // FINISH, finish, 0)

    wait_bytes(rq.at[pl.ds(0, GROUPS - 1)], rq_ss)
    for c in range(CHUNKS):
        wait_bytes(xas[c].at[pl.ds(0, GROUP_BLOCKS - ROWS)], xa_ss.at[c])
        wait_bytes(zs.at[c, pl.ds(0, (GROUPS - 1) * CAP)], z_ss.at[c])
        wait_bytes(xs.at[c, pl.ds(0, PARTS - 1)], xr_ss.at[c])
    for k in range(8):
        w_ring[k].wait_send()
        x_ring[k].wait_send()


def on_device(x, gain, sharp, w3, wf, targets):
    w_own = jnp.transpose(w3, (1, 2, 0)).reshape(3 * WIDTH, 512)
    vmem = pl.BlockSpec(memory_space=pltpu.VMEM)
    smem = pl.BlockSpec(memory_space=pltpu.SMEM)
    dma = pltpu.SemaphoreType.DMA
    sub = pltpu.VMEM((GROUP_BLOCKS, SUB, LANES), BF)
    landed = pltpu.VMEM((GROUPS * CAP, SUB, LANES), BF)
    blocks = pltpu.VMEM((GROUP_BLOCKS, PAIRS, BLK, LANES), BF)
    far_blocks = pltpu.VMEM((PAIRS, ROWS * FAR, BLK, LANES), BF)
    sums = pltpu.VMEM((ROWS, PAIRS, BLK, LANES), F32)
    weights = pltpu.VMEM((2, 512, 2 * LANES), BF)
    attended = pl.pallas_call(
        kernel,
        out_shape=jax.ShapeDtypeStruct(x.shape, BF),
        in_specs=[vmem, vmem, vmem, vmem, smem],
        out_specs=vmem,
        scratch_shapes=[
            pltpu.VMEM((PARTS, ROWS, BLK, 512), BF),
            pltpu.VMEM((PARTS, 3 * WIDTH, 512), BF),
            weights, weights, weights,
            blocks, blocks, far_blocks, far_blocks,
            pltpu.VMEM((ROWS, PAIRS, 2 * BLK, LANES), BF),
            sums, sums,
            sub, sub, sub, sub, landed, landed, landed, landed,
            pltpu.VMEM((CHUNKS, GROUPS * CAP, SUB, LANES), BF),
            pltpu.VMEM((CHUNKS, PARTS, ROWS * FAR, SUB, LANES), BF),
            pltpu.VMEM((PARTS, ROWS * FAR, SUB, 512), BF),
            pltpu.VMEM((2 * 8, LANES), jnp.int32),
            pltpu.VMEM((GROUPS, 1, LANES), jnp.int32),
            pltpu.VMEM((GROUPS, 1, LANES), jnp.int32),
            pltpu.SMEM((GROUPS, 1, LANES), jnp.int32),
            pltpu.VMEM((2 * 8, LANES), jnp.int32),
            pltpu.SMEM((2 * 8, LANES), jnp.int32),
            dma((CHUNKS,)), dma((CHUNKS,)), dma(()), dma(()), dma(()), dma(()),
            dma((8,)), dma((8,)), dma((8,)), dma((8,)),
            dma((CHUNKS,)), dma((CHUNKS,)), dma((CHUNKS,)), dma((CHUNKS,)), dma((PARTS,)),
        ],
        compiler_params=pltpu.CompilerParams(
            collective_id=0, has_side_effects=True, vmem_limit_bytes=60 * 2**20),
        name="block_sparse_layer",
    )(x, gain.reshape(1, 512), w_own, jnp.transpose(targets), sharp)
    return jnp.dot(attended, wf, preferred_element_type=F32).astype(BF)


def solution(mesh):
    placed = (P(("seq", "head"), None), P(), P(), P(None, None, "head"), P(), P("seq", None))
    return jax.shard_map(
        on_device, mesh=mesh, in_specs=placed, out_specs=P(("seq", "head"), None), check_vma=False
    )
```

```python
import math
import jax
import jax.numpy as jnp
from jax import lax
from jax.experimental import pallas as pl
from jax.experimental.pallas import tpu as pltpu
from jax.sharding import PartitionSpec as P

MESH = pl.DeviceIdType.MESH
BF = jnp.bfloat16
F32 = jnp.float32
GROUPS = 32
PARTS = 8
PAIRS = 4
WIDTH = 64
BLK = 128
KB = 12
KL = 10
FAR = 2
CAP = 6
HALF = 3
RING = 8
ROWS = 8
GROUP_BLOCKS = 64
SUB = 16
CHUNKS = 4
LANES = 128
TOGETHER = 4
FINISH = 2
LOG2E = math.log2(math.e)
EPS = 1e-06


def wait_bytes(ref, sem):
    pltpu.make_async_copy(ref, ref, sem).wait()


def kernel(
    x_ref, gain_ref, w_ref, targets_ref, sharp_ref,
    out_ref,
    x_all, w_all, wk, wv, wq, kp, vp, kf, vf, q_all, num, den,
    xa0, xa1, xa2, xa3, zr0, zr1, zr2, zr3a, zr3b,
    x_in, att,
    zs, xs, xs3, xr, xr3, listing, req, rq, rqs, tab, tabs,
    xa_ss, xa_rs, rq_ss, rq_rs, rq_ls, tab_ls, w_ss, w_rs, ag_ss, ag_rs, z_ss, z_rs, xr_ss, xr_rs, far_rs, in_ls, out_ls,
):
    me = lax.axis_index("seq")
    mh = lax.axis_index("head")
    core = lax.rem(mh, 2)
    right = lax.rem(mh + 2, PARTS)
    left = lax.rem(mh + 6, PARTS)
    opp = lax.rem(mh + 4, PARTS)
    sib = mh + 1 - 2 * core
    sib_right = right + 1 - 2 * core
    sib_left = left + 1 - 2 * core
    sib_opp = opp + 1 - 2 * core
    xas = (xa0, xa1, xa2, xa3)
    zrs = (zr0, zr1, zr2, zr3a, zr3b)

    barrier = pltpu.get_barrier_semaphore()
    load_x = pltpu.make_async_copy(x_ref, x_in, in_ls.at[0])
    load_w = pltpu.make_async_copy(w_ref, w_all.at[mh], in_ls.at[1])
    load_x.start()
    load_w.start()

    def greet_seq(d, carry):
        pl.semaphore_signal(barrier, inc=1, device_id={"seq": lax.rem(me + d, GROUPS)}, device_id_type=MESH)
        return carry

    def greet_head(d, carry):
        pl.semaphore_signal(barrier, inc=1, device_id={"head": lax.rem(mh + d, PARTS)}, device_id_type=MESH)
        return carry

    lax.fori_loop(1, GROUPS, greet_seq, 0)
    lax.fori_loop(1, PARTS, greet_head, 0)

    listing[...] = jnp.full(listing.shape, -GROUP_BLOCKS, jnp.int32)
    listing[0:KB, 0:GROUP_BLOCKS] = targets_ref[...]
    lane = lax.broadcasted_iota(jnp.int32, (1, LANES), 1)
    none = jnp.zeros((1, LANES), jnp.int32)
    near_count, far_count = none, none
    near_rows = [none] * KL
    owners, withins = [none] * FAR, [none] * FAR
    for j in range(KB):
        target = listing[j:j + 1, :]
        owner = lax.shift_right_arithmetic(target, 6)
        within = target - owner * GROUP_BLOCKS
        is_far = owner != me
        for k in range(KL):
            near_rows[k] = jnp.where(jnp.logical_and(owner == me, near_count == k), within, near_rows[k])
        for k in range(FAR):
            here = jnp.logical_and(is_far, far_count == k)
            owners[k] = jnp.where(here, owner, owners[k])
            withins[k] = jnp.where(here, within, withins[k])
        near_count = near_count + jnp.where(is_far, 0, 1)
        far_count = far_count + jnp.where(is_far, 1, 0)
    group = lax.broadcasted_iota(jnp.int32, (GROUPS, LANES), 0)
    hits = [jnp.where(group == owners[k], 1, 0) for k in range(FAR)]
    both = hits[0] + hits[1]
    counted = both
    wide_lane = lax.broadcasted_iota(jnp.int32, (GROUPS, LANES), 1)
    for step in (1, 2, 4, 8, 16, 32):
        counted = counted + jnp.where(wide_lane >= step, pltpu.roll(counted, step, 1), 0)
    counted = counted - both

    def over_groups(value):
        eight = value[0:8] + value[8:16] + value[16:24] + value[24:32]
        four = eight[0:4] + eight[4:8]
        two = four[0:2] + four[2:4]
        return two[0:1] + two[1:2]

    slots = [over_groups(hits[0] * counted), over_groups(hits[1] * (counted + hits[0]))]
    wanted = jnp.zeros((GROUPS, LANES), jnp.int32)
    for c in range(CAP):
        one = none
        for k in range(FAR):
            one = one + hits[k] * jnp.where(slots[k] == c, withins[k], 0)
        for step in (1, 2, 4, 8, 16, 32, 64):
            one = one + pltpu.roll(one, step, 1)
        wanted = jnp.where(wide_lane == c, one, wanted)
    for o in range(GROUPS):
        req[o] = wanted[o:o + 1, :]
    rq[me] = req[me]

    pl.semaphore_wait(barrier, GROUPS - 1 + PARTS - 1)

    def send_req(d, carry):
        t = lax.rem(me + d, GROUPS)
        pltpu.make_async_remote_copy(
            src_ref=req.at[t], dst_ref=rq.at[me], send_sem=rq_ss, recv_sem=rq_rs,
            device_id={"seq": t}, device_id_type=MESH,
        ).start()
        return carry

    lax.fori_loop(1, GROUPS, send_req, 0)

    gain = gain_ref[...]

    def norm_block(i, carry):
        rows = x_in[pl.ds(pl.multiple_of(i * BLK, BLK), BLK), :].astype(F32)
        scale = lax.rsqrt(jnp.mean(rows * rows, axis=-1, keepdims=True) + EPS)
        x_all[mh, i] = (rows * scale * gain).astype(BF)
        return carry

    load_x.wait()
    lax.fori_loop(0, ROWS, norm_block, 0)

    def send_sub(c):
        def go(d, carry):
            t = lax.rem(mh + d, PARTS)
            pltpu.make_async_remote_copy(
                src_ref=x_all.at[mh, :, pl.ds(pl.multiple_of(t * SUB, SUB), SUB), pl.ds(c * LANES, LANES)],
                dst_ref=xas[c].at[pl.ds(mh * ROWS, ROWS)],
                send_sem=xa_ss.at[c], recv_sem=xa_rs.at[c],
                device_id={"head": t}, device_id_type=MESH,
            ).start()
            return carry

        lax.fori_loop(1, PARTS, go, 0)
        xas[c][pl.ds(mh * ROWS, ROWS)] = x_all[
            mh, :, pl.ds(pl.multiple_of(mh * SUB, SUB), SUB), pl.ds(c * LANES, LANES)]

    send_sub(0)

    for k in range(KL):
        tab[k:k + 1, :] = near_rows[k]
    for k in range(FAR):
        tab[KL + k:KL + k + 1, :] = owners[k] * CAP + slots[k]
    tab[KB:16, :] = jnp.zeros((16 - KB, LANES), jnp.int32)
    to_tabs = pltpu.make_async_copy(tab, tabs, tab_ls)
    to_tabs.start()

    low = lane < WIDTH
    load_w.wait()

    def ring(buf, ss, rs, half):
        first, second = pl.ds(0, half), pl.ds(half, half)

        def copy(k, view, to):
            return pltpu.make_async_remote_copy(
                src_ref=view, dst_ref=view, send_sem=ss.at[k], recv_sem=rs.at[k],
                device_id={"head": to}, device_id_type=MESH)

        return (
            copy(0, buf.at[mh], right), copy(1, buf.at[mh], left), copy(2, buf.at[mh], sib),
            copy(3, buf.at[left, first], right), copy(4, buf.at[right, second], left),
            copy(5, buf.at[left], sib), copy(6, buf.at[right], sib), copy(7, buf.at[opp], sib),
        )

    w_ring = ring(w_all, w_ss, w_rs, w_all.shape[1] // 2)
    x_ring = ring(x_all, ag_ss, ag_rs, ROWS // 2)

    for k in (0, 1, 2):
        w_ring[k].start()
    for c in range(1, CHUNKS):
        send_sub(c)
    for k in (0, 1, 2):
        x_ring[k].start()

    wait_bytes(rq.at[pl.ds(0, GROUPS - 1)], rq_rs)
    to_smem = pltpu.make_async_copy(rq, rqs, rq_ls)
    to_smem.start()
    to_smem.wait()

    def send_slots(c, k, t, first, count):
        pltpu.make_async_remote_copy(
            src_ref=zs.at[c, pl.ds(first + t * count, count)], dst_ref=zrs[k].at[pl.ds(me * count, count)],
            send_sem=z_ss.at[k], recv_sem=z_rs.at[k],
            device_id={"seq": t}, device_id_type=MESH,
        ).start()

    def send_groups(c):
        wait_bytes(xas[c].at[pl.ds(0, GROUP_BLOCKS - ROWS)], xa_rs.at[c])

        def one(dy, dz):
            t = lax.rem(me // RING + dy, GROUPS // RING) * RING + lax.rem(me + dz, RING)
            if c < CHUNKS - 1:
                for s in range(CAP):
                    zs[c, t * CAP + s] = xas[c][rqs[t, 0, s]]
                send_slots(c, c, t, 0, CAP)
                return
            for s in range(HALF):
                a = xas[c][rqs[t, 0, 2 * s]].astype(F32)
                b = xas[c][rqs[t, 0, 2 * s + 1]].astype(F32)
                zs[c, t * HALF + s] = jnp.concatenate([a[0:8], b[0:8]], axis=0).astype(BF)
                zs[c, GROUPS * HALF + t * HALF + s] = jnp.concatenate([a[8:16], b[8:16]], axis=0).astype(BF)
            send_slots(c, c, t, 0, HALF)

        def go(i, carry):
            dz = jnp.where(i % 2 == 0, 1 + i // 2, RING - 1 - i // 2)
            for dy in (0, 1, 3, 2):
                one(dy, dz)
            return carry

        lax.fori_loop(0, RING - 1, go, 0)
        for dy in (1, 3, 2):
            one(dy, 0)

    def send_rest():
        def one(dy, dz):
            t = lax.rem(me // RING + dy, GROUPS // RING) * RING + lax.rem(me + dz, RING)
            send_slots(CHUNKS - 1, CHUNKS, t, GROUPS * HALF, HALF)

        def go(i, carry):
            dz = jnp.where(i % 2 == 0, 1 + i // 2, RING - 1 - i // 2)
            for dy in (0, 1, 3, 2):
                one(dy, dz)
            return carry

        lax.fori_loop(0, RING - 1, go, 0)
        for dy in (1, 3, 2):
            one(dy, 0)

    send_groups(0)
    w_ring[0].wait_recv()
    w_ring[1].wait_recv()
    for k in (3, 4, 5, 6):
        w_ring[k].start()
    send_groups(1)
    w_ring[3].wait_recv()
    w_ring[4].wait_recv()
    w_ring[7].start()
    send_groups(2)
    send_groups(3)
    send_rest()
    for k in (2, 5, 6, 7):
        w_ring[k].wait_recv()
    to_tabs.wait()

    for k, ref in enumerate((wq, wk, wv)):
        for t in range(2):
            ref[t] = jnp.transpose(
                jnp.concatenate([w_all[4 * t + n, k * WIDTH:(k + 1) * WIDTH] for n in range(4)], axis=0), (1, 0))

    row2 = lax.broadcasted_iota(jnp.int32, (2 * LANES, 2 * LANES), 0)
    col2 = lax.broadcasted_iota(jnp.int32, (2 * LANES, 2 * LANES), 1)
    spread = jnp.where(row2 // WIDTH == col2 // WIDTH, 1.0 / WIDTH, 0.0).astype(BF)

    def unit_rows(rows, weights):
        wide = jnp.dot(rows, weights, preferred_element_type=F32).astype(BF).astype(F32)
        mean = jnp.dot((wide * wide).astype(BF), spread, preferred_element_type=F32)
        return (wide * lax.rsqrt(mean + EPS)).astype(BF)

    def plain_rows(rows, weights):
        return jnp.dot(rows, weights, preferred_element_type=F32).astype(BF)

    def project(s):
        def go(i, carry):
            rows = x_all[s, pl.ds(TOGETHER * i, TOGETHER)].reshape(TOGETHER * BLK, 512)
            for t in range(2):
                for ref, both in ((kp, unit_rows(rows, wk[t])), (vp, plain_rows(rows, wv[t]))):
                    for n in range(2):
                        for m in range(TOGETHER):
                            ref[s * ROWS + TOGETHER * i + m, 2 * t + n] = both[
                                m * BLK:(m + 1) * BLK, n * LANES:(n + 1) * LANES]
            return carry

        lax.fori_loop(0, ROWS // TOGETHER, go, 0)

    def project_queries():
        def go(i, carry):
            rows = x_all[mh, pl.ds(TOGETHER * i, TOGETHER)].reshape(TOGETHER * BLK, 512)
            for t in range(2):
                both = unit_rows(rows, wq[t])
                for n in range(2):
                    for m in range(TOGETHER):
                        one = both[m * BLK:(m + 1) * BLK, n * LANES:(n + 1) * LANES]
                        none = jnp.zeros_like(one)
                        q_all[TOGETHER * i + m, 2 * t + n, 0:BLK] = jnp.where(low, one, none)
                        q_all[TOGETHER * i + m, 2 * t + n, BLK:2 * BLK] = jnp.where(low, none, one)
            return carry

        lax.fori_loop(0, ROWS // TOGETHER, go, 0)

    def score(q, keys):
        return lax.dot_general(q, keys, (((1,), (1,)), ((), ())), preferred_element_type=F32)

    def blend(scores, values, p):
        weights = []
        for n in range(2):
            sharp = sharp_ref[2 * p + n]
            weights.append(jnp.exp2(
                scores[n * BLK:(n + 1) * BLK] * (sharp * (LOG2E / WIDTH)) - sharp * LOG2E).astype(BF))
        values = jnp.concatenate([values, jnp.ones_like(values)], axis=1)
        return jnp.dot(jnp.concatenate(weights, axis=0), values, preferred_element_type=F32)

    def parted(both):
        return (jnp.where(low, both[0:BLK, 0:LANES], both[BLK:2 * BLK, 0:LANES]),
                jnp.where(low, both[0:BLK, LANES:2 * LANES], both[BLK:2 * BLK, LANES:2 * LANES]))

    def near(first, last):
        def go(b, carry):
            listed = [tabs[j, mh * ROWS + b] for j in range(KL)]
            scores = [
                score(q_all[b, p], jnp.concatenate([kp[i, p] for i in listed], axis=0)) for p in range(PAIRS)]
            for p in range(PAIRS):
                both = blend(scores[p], jnp.concatenate([vp[i, p] for i in listed], axis=0), p)
                num[b, p], den[b, p] = parted(both)
            return carry

        lax.fori_loop(first, last, go, 0)

    def pass_on(k):
        c, half = (k, 0) if k < CHUNKS else (CHUNKS - 1, 1)
        halved = c == CHUNKS - 1
        count = HALF if halved else CAP
        wait_bytes(zrs[k].at[pl.ds(0, (GROUPS - 1) * count)], z_rs.at[k])

        def part(t, b, j):
            place = tabs[KL + j, t * ROWS + b]
            both = zrs[k][lax.shift_right_arithmetic(place, 1)].astype(F32)
            upper = jnp.full((8, LANES), place & 1, jnp.int32) == 0
            return jnp.where(upper, both[0:8], both[8:16])

        def go(i, carry):
            t = lax.rem(mh + jnp.where(i % 2 == 0, 4 + i // 2, 3 - i // 2), PARTS)
            if halved:
                for b in range(ROWS):
                    xs3[half, t, b] = jnp.concatenate([part(t, b, 0), part(t, b, 1)], axis=0).astype(BF)
                src, dst = xs3.at[half, t], xr3.at[half, mh]
            else:
                for e in range(ROWS * FAR):
                    xs[c, t, e] = zrs[c][tabs[KL + e % FAR, t * ROWS + e // FAR]]
                src, dst = xs.at[c, t], xr.at[mh, :, :, pl.ds(c * LANES, LANES)]

            @pl.when(i < PARTS - 1)
            def _():
                pltpu.make_async_remote_copy(
                    src_ref=src, dst_ref=dst,
                    send_sem=xr_ss.at[k], recv_sem=xr_rs.at[k] if k < CHUNKS else far_rs.at[mh],
                    device_id={"head": t}, device_id_type=MESH,
                ).start()

            return carry

        lax.fori_loop(0, PARTS, go, 0)
        if halved:
            xr3[half, mh] = xs3[half, mh]
        else:
            xr[mh, :, :, pl.ds(c * LANES, LANES)] = xs[c, mh]

    project(mh)
    x_ring[0].wait_recv()
    x_ring[1].wait_recv()
    for k in (3, 4, 5, 6):
        x_ring[k].start()
    x_ring[2].wait_recv()
    project(sib)
    project_queries()
    project(left)
    project(right)
    pass_on(0)
    x_ring[3].wait_recv()
    x_ring[4].wait_recv()
    x_ring[7].start()
    project(opp)
    x_ring[5].wait_recv()
    project(sib_left)
    x_ring[6].wait_recv()
    project(sib_right)
    pass_on(1)
    x_ring[7].wait_recv()
    project(sib_opp)
    pass_on(2)
    near(0, 4)
    pass_on(3)
    near(4, 6)
    pass_on(4)
    near(6, ROWS)
    for c in range(CHUNKS - 1):
        wait_bytes(xs.at[c, pl.ds(0, PARTS - 1)], xr_rs.at[c])
    wait_bytes(xs3.at[0, pl.ds(0, PARTS - 1)], xr_rs.at[CHUNKS - 1])

    sources = (mh, sib, left, right, sib_left, sib_right, opp, sib_opp)

    def project_far(k):
        count = ROWS * FAR * SUB
        for s in sources[k:k + 2]:
            if s is not mh:
                wait_bytes(xs3.at[1, 0], far_rs.at[s])
            first, second = xr3[0, s].astype(F32), xr3[1, s].astype(F32)
            rows = [jnp.concatenate([first[:, r:r + 8], second[:, r:r + 8]], axis=1) for r in (0, 8)]
            xr[s, :, :, pl.ds((CHUNKS - 1) * LANES, LANES)] = jnp.stack(rows, axis=1).reshape(
                ROWS * FAR, SUB, LANES).astype(BF)
        rows = jnp.concatenate([xr[s].reshape(count, 512) for s in sources[k:k + 2]], axis=0)
        for t in range(2):
            for ref, both in ((kf, unit_rows(rows, wk[t])), (vf, plain_rows(rows, wv[t]))):
                for n in range(2):
                    for m in range(2):
                        ref[2 * t + n, :, (k + m) * SUB:(k + m + 1) * SUB, :] = both[
                            m * count:(m + 1) * count, n * LANES:(n + 1) * LANES].reshape(ROWS * FAR, SUB, LANES)

    def far_keys(ref, b, p):
        return ref[p, pl.ds(FAR * b, FAR)].reshape(FAR * BLK, LANES)

    def store(i):
        rows = pl.ds(pl.multiple_of(i * FINISH * BLK, FINISH * BLK), FINISH * BLK)
        return pltpu.make_async_copy(att.at[rows], out_ref.at[rows], out_ls.at[i])

    def finish(i, carry):
        units = [(FINISH * i + m, p) for m in range(FINISH) for p in range(PAIRS)]
        scores = [score(q_all[b, p], far_keys(kf, b, p)) for b, p in units]
        for (b, p), one in zip(units, scores):
            top, bottom = parted(blend(one, far_keys(vf, b, p), p))
            att[pl.ds(pl.multiple_of(b * BLK, BLK), BLK), p * LANES:(p + 1) * LANES] = (
                (num[b, p] + top) / (den[b, p] + bottom)).astype(BF)
        store(i).start()
        return carry

    for k in range(0, PARTS, 2):
        project_far(k)
    lax.fori_loop(0, ROWS // FINISH, finish, 0)

    wait_bytes(rq.at[pl.ds(0, GROUPS - 1)], rq_ss)
    for c in range(CHUNKS):
        wait_bytes(xas[c].at[pl.ds(0, GROUP_BLOCKS - ROWS)], xa_ss.at[c])
        if c < CHUNKS - 1:
            wait_bytes(zs.at[c, pl.ds(0, (GROUPS - 1) * CAP)], z_ss.at[c])
            wait_bytes(xs.at[c, pl.ds(0, PARTS - 1)], xr_ss.at[c])
    for k in (CHUNKS - 1, CHUNKS):
        wait_bytes(zs.at[0, pl.ds(0, (GROUPS - 1) * HALF)], z_ss.at[k])
        wait_bytes(xs3.at[0, pl.ds(0, PARTS - 1)], xr_ss.at[k])
    for i in range(ROWS // FINISH):
        store(i).wait()
    for k in range(8):
        w_ring[k].wait_send()
        x_ring[k].wait_send()


def on_device(x, gain, sharp, w3, wf, targets):
    w_own = jnp.transpose(w3, (1, 2, 0)).reshape(3 * WIDTH, 512)
    vmem = pl.BlockSpec(memory_space=pltpu.VMEM)
    smem = pl.BlockSpec(memory_space=pltpu.SMEM)
    hbm = pl.BlockSpec(memory_space=pl.ANY)
    dma = pltpu.SemaphoreType.DMA
    sub = pltpu.VMEM((GROUP_BLOCKS, SUB, LANES), BF)
    landed = pltpu.VMEM((GROUPS * CAP, SUB, LANES), BF)
    half_landed = pltpu.VMEM((GROUPS * HALF, SUB, LANES), BF)
    blocks = pltpu.VMEM((GROUP_BLOCKS, PAIRS, BLK, LANES), BF)
    far_blocks = pltpu.VMEM((PAIRS, ROWS * FAR, BLK, LANES), BF)
    sums = pltpu.VMEM((ROWS, PAIRS, BLK, LANES), F32)
    weights = pltpu.VMEM((2, 512, 2 * LANES), BF)
    attended = pl.pallas_call(
        kernel,
        out_shape=jax.ShapeDtypeStruct(x.shape, BF),
        in_specs=[hbm, vmem, hbm, vmem, smem],
        out_specs=hbm,
        scratch_shapes=[
            pltpu.VMEM((PARTS, ROWS, BLK, 512), BF),
            pltpu.VMEM((PARTS, 3 * WIDTH, 512), BF),
            weights, weights, weights,
            blocks, blocks, far_blocks, far_blocks,
            pltpu.VMEM((ROWS, PAIRS, 2 * BLK, LANES), BF),
            sums, sums,
            sub, sub, sub, sub, landed, landed, landed, half_landed, half_landed,
            pltpu.VMEM(x.shape, BF), pltpu.VMEM(x.shape, BF),
            pltpu.VMEM((CHUNKS, GROUPS * CAP, SUB, LANES), BF),
            pltpu.VMEM((CHUNKS - 1, PARTS, ROWS * FAR, SUB, LANES), BF),
            pltpu.VMEM((2, PARTS, ROWS, SUB, LANES), BF),
            pltpu.VMEM((PARTS, ROWS * FAR, SUB, 512), BF),
            pltpu.VMEM((2, PARTS, ROWS, SUB, LANES), BF),
            pltpu.VMEM((2 * 8, LANES), jnp.int32),
            pltpu.VMEM((GROUPS, 1, LANES), jnp.int32),
            pltpu.VMEM((GROUPS, 1, LANES), jnp.int32),
            pltpu.SMEM((GROUPS, 1, LANES), jnp.int32),
            pltpu.VMEM((2 * 8, LANES), jnp.int32),
            pltpu.SMEM((2 * 8, LANES), jnp.int32),
            dma((CHUNKS,)), dma((CHUNKS,)), dma(()), dma(()), dma(()), dma(()),
            dma((8,)), dma((8,)), dma((8,)), dma((8,)),
            dma((CHUNKS + 1,)), dma((CHUNKS + 1,)), dma((CHUNKS + 1,)), dma((CHUNKS,)), dma((PARTS,)),
            dma((2,)), dma((ROWS // FINISH,)),
        ],
        compiler_params=pltpu.CompilerParams(
            collective_id=0, has_side_effects=True, vmem_limit_bytes=60 * 2**20),
        name="block_sparse_layer",
    )(x, gain.reshape(1, 512), w_own, jnp.transpose(targets), sharp)
    return jnp.dot(attended, wf, preferred_element_type=F32).astype(BF)


def solution(mesh):
    placed = (P(("seq", "head"), None), P(), P(), P(None, None, "head"), P(), P("seq", None))
    return jax.shard_map(
        on_device, mesh=mesh, in_specs=placed, out_specs=P(("seq", "head"), None), check_vma=False
    )
```

```python
import math
import jax
import jax.numpy as jnp
from jax import lax
from jax.experimental import pallas as pl
from jax.experimental.pallas import tpu as pltpu
from jax.sharding import PartitionSpec as P

MESH = pl.DeviceIdType.MESH
BF = jnp.bfloat16
F32 = jnp.float32
GROUPS = 32
PARTS = 8
PAIRS = 4
WIDTH = 64
BLK = 128
KB = 12
KL = 10
FAR = 2
CAP = 6
HALF = 3
RING = 8
ROWS = 8
GROUP_BLOCKS = 64
SUB = 16
CHUNKS = 4
LANES = 128
TOGETHER = 4
FINISH = 2
LOG2E = math.log2(math.e)
EPS = 1e-06


def wait_bytes(ref, sem):
    pltpu.make_async_copy(ref, ref, sem).wait()


def kernel(
    x_ref, gain_ref, w_ref, targets_ref, sharp_ref,
    out_ref,
    x_all, w_all, wk, wv, wq, kp, vp, kf, vf, q_all, num, den,
    xa0, xa1, xa2, xa3, zr0, zr1, zr2, zr3a, zr3b,
    x_in,
    zs, xs, xs3, xr, xr3, listing, req, rq, rqs, tab, tabs,
    xa_ss, xa_rs, rq_ss, rq_rs, rq_ls, tab_ls, w_ss, w_rs, ag_ss, ag_rs, z_ss, z_rs, xr_ss, xr_rs, far_rs, in_ls,
):
    me = lax.axis_index("seq")
    mh = lax.axis_index("head")
    core = lax.rem(mh, 2)
    right = lax.rem(mh + 2, PARTS)
    left = lax.rem(mh + 6, PARTS)
    opp = lax.rem(mh + 4, PARTS)
    sib = mh + 1 - 2 * core
    sib_right = right + 1 - 2 * core
    sib_left = left + 1 - 2 * core
    sib_opp = opp + 1 - 2 * core
    xas = (xa0, xa1, xa2, xa3)
    zrs = (zr0, zr1, zr2, zr3a, zr3b)

    barrier = pltpu.get_barrier_semaphore()
    load_x = pltpu.make_async_copy(x_ref, x_in, in_ls.at[0])
    load_w = pltpu.make_async_copy(w_ref, w_all.at[mh], in_ls.at[1])
    load_x.start()
    load_w.start()

    def greet_seq(d, carry):
        pl.semaphore_signal(barrier, inc=1, device_id={"seq": lax.rem(me + d, GROUPS)}, device_id_type=MESH)
        return carry

    def greet_head(d, carry):
        pl.semaphore_signal(barrier, inc=1, device_id={"head": lax.rem(mh + d, PARTS)}, device_id_type=MESH)
        return carry

    lax.fori_loop(1, GROUPS, greet_seq, 0)
    lax.fori_loop(1, PARTS, greet_head, 0)

    listing[...] = jnp.full(listing.shape, -GROUP_BLOCKS, jnp.int32)
    listing[0:KB, 0:GROUP_BLOCKS] = targets_ref[...]
    lane = lax.broadcasted_iota(jnp.int32, (1, LANES), 1)
    none = jnp.zeros((1, LANES), jnp.int32)
    near_count, far_count = none, none
    near_rows = [none] * KL
    owners, withins = [none] * FAR, [none] * FAR
    for j in range(KB):
        target = listing[j:j + 1, :]
        owner = lax.shift_right_arithmetic(target, 6)
        within = target - owner * GROUP_BLOCKS
        is_far = owner != me
        for k in range(KL):
            near_rows[k] = jnp.where(jnp.logical_and(owner == me, near_count == k), within, near_rows[k])
        for k in range(FAR):
            here = jnp.logical_and(is_far, far_count == k)
            owners[k] = jnp.where(here, owner, owners[k])
            withins[k] = jnp.where(here, within, withins[k])
        near_count = near_count + jnp.where(is_far, 0, 1)
        far_count = far_count + jnp.where(is_far, 1, 0)
    group = lax.broadcasted_iota(jnp.int32, (GROUPS, LANES), 0)
    hits = [jnp.where(group == owners[k], 1, 0) for k in range(FAR)]
    both = hits[0] + hits[1]
    counted = both
    wide_lane = lax.broadcasted_iota(jnp.int32, (GROUPS, LANES), 1)
    for step in (1, 2, 4, 8, 16, 32):
        counted = counted + jnp.where(wide_lane >= step, pltpu.roll(counted, step, 1), 0)
    counted = counted - both

    def over_groups(value):
        eight = value[0:8] + value[8:16] + value[16:24] + value[24:32]
        four = eight[0:4] + eight[4:8]
        two = four[0:2] + four[2:4]
        return two[0:1] + two[1:2]

    slots = [over_groups(hits[0] * counted), over_groups(hits[1] * (counted + hits[0]))]
    wanted = jnp.zeros((GROUPS, LANES), jnp.int32)
    for c in range(CAP):
        one = none
        for k in range(FAR):
            one = one + hits[k] * jnp.where(slots[k] == c, withins[k], 0)
        for step in (1, 2, 4, 8, 16, 32, 64):
            one = one + pltpu.roll(one, step, 1)
        wanted = jnp.where(wide_lane == c, one, wanted)
    for o in range(GROUPS):
        req[o] = wanted[o:o + 1, :]
    rq[me] = req[me]

    pl.semaphore_wait(barrier, GROUPS - 1 + PARTS - 1)

    def send_req(d, carry):
        t = lax.rem(me + d, GROUPS)
        pltpu.make_async_remote_copy(
            src_ref=req.at[t], dst_ref=rq.at[me], send_sem=rq_ss, recv_sem=rq_rs,
            device_id={"seq": t}, device_id_type=MESH,
        ).start()
        return carry

    lax.fori_loop(1, GROUPS, send_req, 0)

    gain = gain_ref[...]

    def norm_block(i, carry):
        rows = x_in[pl.ds(pl.multiple_of(i * BLK, BLK), BLK), :].astype(F32)
        scale = lax.rsqrt(jnp.mean(rows * rows, axis=-1, keepdims=True) + EPS)
        x_all[mh, i] = (rows * scale * gain).astype(BF)
        return carry

    load_x.wait()
    lax.fori_loop(0, ROWS, norm_block, 0)

    def send_sub(c):
        def go(d, carry):
            t = lax.rem(mh + d, PARTS)
            pltpu.make_async_remote_copy(
                src_ref=x_all.at[mh, :, pl.ds(pl.multiple_of(t * SUB, SUB), SUB), pl.ds(c * LANES, LANES)],
                dst_ref=xas[c].at[pl.ds(mh * ROWS, ROWS)],
                send_sem=xa_ss.at[c], recv_sem=xa_rs.at[c],
                device_id={"head": t}, device_id_type=MESH,
            ).start()
            return carry

        lax.fori_loop(1, PARTS, go, 0)
        xas[c][pl.ds(mh * ROWS, ROWS)] = x_all[
            mh, :, pl.ds(pl.multiple_of(mh * SUB, SUB), SUB), pl.ds(c * LANES, LANES)]

    send_sub(0)

    for k in range(KL):
        tab[k:k + 1, :] = near_rows[k]
    for k in range(FAR):
        tab[KL + k:KL + k + 1, :] = owners[k] * CAP + slots[k]
    tab[KB:16, :] = jnp.zeros((16 - KB, LANES), jnp.int32)
    to_tabs = pltpu.make_async_copy(tab, tabs, tab_ls)
    to_tabs.start()

    low = lane < WIDTH
    load_w.wait()

    def ring(buf, ss, rs, half):
        first, second = pl.ds(0, half), pl.ds(half, half)

        def copy(k, view, to):
            return pltpu.make_async_remote_copy(
                src_ref=view, dst_ref=view, send_sem=ss.at[k], recv_sem=rs.at[k],
                device_id={"head": to}, device_id_type=MESH)

        return (
            copy(0, buf.at[mh], right), copy(1, buf.at[mh], left), copy(2, buf.at[mh], sib),
            copy(3, buf.at[left, first], right), copy(4, buf.at[right, second], left),
            copy(5, buf.at[left], sib), copy(6, buf.at[right], sib), copy(7, buf.at[opp], sib),
        )

    w_ring = ring(w_all, w_ss, w_rs, w_all.shape[1] // 2)
    x_ring = ring(x_all, ag_ss, ag_rs, ROWS // 2)

    for k in (0, 1, 2):
        w_ring[k].start()
    for c in range(1, CHUNKS):
        send_sub(c)
    for k in (0, 1, 2):
        x_ring[k].start()

    wait_bytes(rq.at[pl.ds(0, GROUPS - 1)], rq_rs)
    to_smem = pltpu.make_async_copy(rq, rqs, rq_ls)
    to_smem.start()
    to_smem.wait()

    def send_slots(c, k, t, first, count):
        pltpu.make_async_remote_copy(
            src_ref=zs.at[c, pl.ds(first + t * count, count)], dst_ref=zrs[k].at[pl.ds(me * count, count)],
            send_sem=z_ss.at[k], recv_sem=z_rs.at[k],
            device_id={"seq": t}, device_id_type=MESH,
        ).start()

    def send_groups(c):
        wait_bytes(xas[c].at[pl.ds(0, GROUP_BLOCKS - ROWS)], xa_rs.at[c])

        def one(dy, dz):
            t = lax.rem(me // RING + dy, GROUPS // RING) * RING + lax.rem(me + dz, RING)
            if c < CHUNKS - 1:
                for s in range(CAP):
                    zs[c, t * CAP + s] = xas[c][rqs[t, 0, s]]
                send_slots(c, c, t, 0, CAP)
                return
            for s in range(HALF):
                a = xas[c][rqs[t, 0, 2 * s]].astype(F32)
                b = xas[c][rqs[t, 0, 2 * s + 1]].astype(F32)
                zs[c, t * HALF + s] = jnp.concatenate([a[0:8], b[0:8]], axis=0).astype(BF)
                zs[c, GROUPS * HALF + t * HALF + s] = jnp.concatenate([a[8:16], b[8:16]], axis=0).astype(BF)
            send_slots(c, c, t, 0, HALF)

        def go(i, carry):
            dz = jnp.where(i % 2 == 0, 1 + i // 2, RING - 1 - i // 2)
            for dy in (0, 1, 3, 2):
                one(dy, dz)
            return carry

        lax.fori_loop(0, RING - 1, go, 0)
        for dy in (1, 3, 2):
            one(dy, 0)

    def send_rest():
        def one(dy, dz):
            t = lax.rem(me // RING + dy, GROUPS // RING) * RING + lax.rem(me + dz, RING)
            send_slots(CHUNKS - 1, CHUNKS, t, GROUPS * HALF, HALF)

        def go(i, carry):
            dz = jnp.where(i % 2 == 0, 1 + i // 2, RING - 1 - i // 2)
            for dy in (0, 1, 3, 2):
                one(dy, dz)
            return carry

        lax.fori_loop(0, RING - 1, go, 0)
        for dy in (1, 3, 2):
            one(dy, 0)

    send_groups(0)
    w_ring[0].wait_recv()
    w_ring[1].wait_recv()
    for k in (3, 4, 5, 6):
        w_ring[k].start()
    send_groups(1)
    w_ring[3].wait_recv()
    w_ring[4].wait_recv()
    w_ring[7].start()
    send_groups(2)
    send_groups(3)
    send_rest()
    for k in (2, 5, 6, 7):
        w_ring[k].wait_recv()
    to_tabs.wait()

    for k, ref in enumerate((wq, wk, wv)):
        for t in range(2):
            ref[t] = jnp.transpose(
                jnp.concatenate([w_all[4 * t + n, k * WIDTH:(k + 1) * WIDTH] for n in range(4)], axis=0), (1, 0))

    row2 = lax.broadcasted_iota(jnp.int32, (2 * LANES, 2 * LANES), 0)
    col2 = lax.broadcasted_iota(jnp.int32, (2 * LANES, 2 * LANES), 1)
    spread = jnp.where(row2 // WIDTH == col2 // WIDTH, 1.0 / WIDTH, 0.0).astype(BF)

    def unit_rows(rows, weights):
        wide = jnp.dot(rows, weights, preferred_element_type=F32).astype(BF).astype(F32)
        mean = jnp.dot((wide * wide).astype(BF), spread, preferred_element_type=F32)
        return (wide * lax.rsqrt(mean + EPS)).astype(BF)

    def plain_rows(rows, weights):
        return jnp.dot(rows, weights, preferred_element_type=F32).astype(BF)

    def project(s):
        def go(i, carry):
            rows = x_all[s, pl.ds(TOGETHER * i, TOGETHER)].reshape(TOGETHER * BLK, 512)
            for t in range(2):
                for ref, both in ((kp, unit_rows(rows, wk[t])), (vp, plain_rows(rows, wv[t]))):
                    for n in range(2):
                        for m in range(TOGETHER):
                            ref[s * ROWS + TOGETHER * i + m, 2 * t + n] = both[
                                m * BLK:(m + 1) * BLK, n * LANES:(n + 1) * LANES]
            return carry

        lax.fori_loop(0, ROWS // TOGETHER, go, 0)

    def project_queries():
        def go(i, carry):
            rows = x_all[mh, pl.ds(TOGETHER * i, TOGETHER)].reshape(TOGETHER * BLK, 512)
            for t in range(2):
                both = unit_rows(rows, wq[t])
                for n in range(2):
                    for m in range(TOGETHER):
                        one = both[m * BLK:(m + 1) * BLK, n * LANES:(n + 1) * LANES]
                        none = jnp.zeros_like(one)
                        q_all[TOGETHER * i + m, 2 * t + n, 0:BLK] = jnp.where(low, one, none)
                        q_all[TOGETHER * i + m, 2 * t + n, BLK:2 * BLK] = jnp.where(low, none, one)
            return carry

        lax.fori_loop(0, ROWS // TOGETHER, go, 0)

    def score(q, keys):
        return lax.dot_general(q, keys, (((1,), (1,)), ((), ())), preferred_element_type=F32)

    def blend(scores, values, p):
        weights = []
        for n in range(2):
            sharp = sharp_ref[2 * p + n]
            weights.append(jnp.exp2(
                scores[n * BLK:(n + 1) * BLK] * (sharp * (LOG2E / WIDTH)) - sharp * LOG2E).astype(BF))
        values = jnp.concatenate([values, jnp.ones_like(values)], axis=1)
        return jnp.dot(jnp.concatenate(weights, axis=0), values, preferred_element_type=F32)

    def parted(both):
        return (jnp.where(low, both[0:BLK, 0:LANES], both[BLK:2 * BLK, 0:LANES]),
                jnp.where(low, both[0:BLK, LANES:2 * LANES], both[BLK:2 * BLK, LANES:2 * LANES]))

    def near(first, last):
        def go(b, carry):
            listed = [tabs[j, mh * ROWS + b] for j in range(KL)]
            scores = [
                score(q_all[b, p], jnp.concatenate([kp[i, p] for i in listed], axis=0)) for p in range(PAIRS)]
            for p in range(PAIRS):
                both = blend(scores[p], jnp.concatenate([vp[i, p] for i in listed], axis=0), p)
                num[b, p], den[b, p] = parted(both)
            return carry

        lax.fori_loop(first, last, go, 0)

    def pass_on(k):
        c, half = (k, 0) if k < CHUNKS else (CHUNKS - 1, 1)
        halved = c == CHUNKS - 1
        count = HALF if halved else CAP
        wait_bytes(zrs[k].at[pl.ds(0, (GROUPS - 1) * count)], z_rs.at[k])

        def part(t, b, j):
            place = tabs[KL + j, t * ROWS + b]
            both = zrs[k][lax.shift_right_arithmetic(place, 1)].astype(F32)
            upper = jnp.full((8, LANES), place & 1, jnp.int32) == 0
            return jnp.where(upper, both[0:8], both[8:16])

        def go(i, carry):
            t = lax.rem(mh + jnp.where(i % 2 == 0, 4 + i // 2, 3 - i // 2), PARTS)
            if halved:
                for b in range(ROWS):
                    xs3[half, t, b] = jnp.concatenate([part(t, b, 0), part(t, b, 1)], axis=0).astype(BF)
                src, dst = xs3.at[half, t], xr3.at[half, mh]
            else:
                for e in range(ROWS * FAR):
                    xs[c, t, e] = zrs[c][tabs[KL + e % FAR, t * ROWS + e // FAR]]
                src, dst = xs.at[c, t], xr.at[mh, :, :, pl.ds(c * LANES, LANES)]

            @pl.when(i < PARTS - 1)
            def _():
                pltpu.make_async_remote_copy(
                    src_ref=src, dst_ref=dst,
                    send_sem=xr_ss.at[k], recv_sem=xr_rs.at[k] if k < CHUNKS else far_rs.at[mh],
                    device_id={"head": t}, device_id_type=MESH,
                ).start()

            return carry

        lax.fori_loop(0, PARTS, go, 0)
        if halved:
            xr3[half, mh] = xs3[half, mh]
        else:
            xr[mh, :, :, pl.ds(c * LANES, LANES)] = xs[c, mh]

    project(mh)
    x_ring[0].wait_recv()
    x_ring[1].wait_recv()
    for k in (3, 4, 5, 6):
        x_ring[k].start()
    x_ring[2].wait_recv()
    project(sib)
    project_queries()
    project(left)
    project(right)
    pass_on(0)
    x_ring[3].wait_recv()
    x_ring[4].wait_recv()
    x_ring[7].start()
    project(opp)
    x_ring[5].wait_recv()
    project(sib_left)
    x_ring[6].wait_recv()
    project(sib_right)
    pass_on(1)
    x_ring[7].wait_recv()
    project(sib_opp)
    pass_on(2)
    near(0, 4)
    pass_on(3)
    near(4, 6)
    pass_on(4)
    near(6, ROWS)
    for c in range(CHUNKS - 1):
        wait_bytes(xs.at[c, pl.ds(0, PARTS - 1)], xr_rs.at[c])
    wait_bytes(xs3.at[0, pl.ds(0, PARTS - 1)], xr_rs.at[CHUNKS - 1])

    sources = (mh, sib, left, right, sib_left, sib_right, opp, sib_opp)

    def project_far(k):
        count = ROWS * FAR * SUB
        for s in sources[k:k + 2]:
            if s is not mh:
                wait_bytes(xs3.at[1, 0], far_rs.at[s])
            first, second = xr3[0, s].astype(F32), xr3[1, s].astype(F32)
            rows = [jnp.concatenate([first[:, r:r + 8], second[:, r:r + 8]], axis=1) for r in (0, 8)]
            xr[s, :, :, pl.ds((CHUNKS - 1) * LANES, LANES)] = jnp.stack(rows, axis=1).reshape(
                ROWS * FAR, SUB, LANES).astype(BF)
        rows = jnp.concatenate([xr[s].reshape(count, 512) for s in sources[k:k + 2]], axis=0)
        for t in range(2):
            for ref, both in ((kf, unit_rows(rows, wk[t])), (vf, plain_rows(rows, wv[t]))):
                for n in range(2):
                    for m in range(2):
                        ref[2 * t + n, :, (k + m) * SUB:(k + m + 1) * SUB, :] = both[
                            m * count:(m + 1) * count, n * LANES:(n + 1) * LANES].reshape(ROWS * FAR, SUB, LANES)

    def far_keys(ref, b, p):
        return ref[p, pl.ds(FAR * b, FAR)].reshape(FAR * BLK, LANES)

    def finish(i, carry):
        units = [(FINISH * i + m, p) for m in range(FINISH) for p in range(PAIRS)]
        scores = [score(q_all[b, p], far_keys(kf, b, p)) for b, p in units]
        for (b, p), one in zip(units, scores):
            top, bottom = parted(blend(one, far_keys(vf, b, p), p))
            out_ref[pl.ds(pl.multiple_of(b * BLK, BLK), BLK), p * LANES:(p + 1) * LANES] = (
                (num[b, p] + top) / (den[b, p] + bottom)).astype(BF)
        return carry

    for k in range(0, PARTS, 2):
        project_far(k)
    lax.fori_loop(0, ROWS // FINISH, finish, 0)

    wait_bytes(rq.at[pl.ds(0, GROUPS - 1)], rq_ss)
    for c in range(CHUNKS):
        wait_bytes(xas[c].at[pl.ds(0, GROUP_BLOCKS - ROWS)], xa_ss.at[c])
        if c < CHUNKS - 1:
            wait_bytes(zs.at[c, pl.ds(0, (GROUPS - 1) * CAP)], z_ss.at[c])
            wait_bytes(xs.at[c, pl.ds(0, PARTS - 1)], xr_ss.at[c])
    for k in (CHUNKS - 1, CHUNKS):
        wait_bytes(zs.at[0, pl.ds(0, (GROUPS - 1) * HALF)], z_ss.at[k])
        wait_bytes(xs3.at[0, pl.ds(0, PARTS - 1)], xr_ss.at[k])
    for k in range(8):
        w_ring[k].wait_send()
        x_ring[k].wait_send()


def on_device(x, gain, sharp, w3, wf, targets):
    w_own = jnp.transpose(w3, (1, 2, 0)).reshape(3 * WIDTH, 512)
    vmem = pl.BlockSpec(memory_space=pltpu.VMEM)
    smem = pl.BlockSpec(memory_space=pltpu.SMEM)
    hbm = pl.BlockSpec(memory_space=pl.ANY)
    dma = pltpu.SemaphoreType.DMA
    sub = pltpu.VMEM((GROUP_BLOCKS, SUB, LANES), BF)
    landed = pltpu.VMEM((GROUPS * CAP, SUB, LANES), BF)
    half_landed = pltpu.VMEM((GROUPS * HALF, SUB, LANES), BF)
    blocks = pltpu.VMEM((GROUP_BLOCKS, PAIRS, BLK, LANES), BF)
    far_blocks = pltpu.VMEM((PAIRS, ROWS * FAR, BLK, LANES), BF)
    sums = pltpu.VMEM((ROWS, PAIRS, BLK, LANES), F32)
    weights = pltpu.VMEM((2, 512, 2 * LANES), BF)
    attended = pl.pallas_call(
        kernel,
        out_shape=pltpu.VMEM(x.shape, BF),
        in_specs=[hbm, vmem, hbm, vmem, smem],
        out_specs=vmem,
        scratch_shapes=[
            pltpu.VMEM((PARTS, ROWS, BLK, 512), BF),
            pltpu.VMEM((PARTS, 3 * WIDTH, 512), BF),
            weights, weights, weights,
            blocks, blocks, far_blocks, far_blocks,
            pltpu.VMEM((ROWS, PAIRS, 2 * BLK, LANES), BF),
            sums, sums,
            sub, sub, sub, sub, landed, landed, landed, half_landed, half_landed,
            pltpu.VMEM(x.shape, BF),
            pltpu.VMEM((CHUNKS, GROUPS * CAP, SUB, LANES), BF),
            pltpu.VMEM((CHUNKS - 1, PARTS, ROWS * FAR, SUB, LANES), BF),
            pltpu.VMEM((2, PARTS, ROWS, SUB, LANES), BF),
            pltpu.VMEM((PARTS, ROWS * FAR, SUB, 512), BF),
            pltpu.VMEM((2, PARTS, ROWS, SUB, LANES), BF),
            pltpu.VMEM((2 * 8, LANES), jnp.int32),
            pltpu.VMEM((GROUPS, 1, LANES), jnp.int32),
            pltpu.VMEM((GROUPS, 1, LANES), jnp.int32),
            pltpu.SMEM((GROUPS, 1, LANES), jnp.int32),
            pltpu.VMEM((2 * 8, LANES), jnp.int32),
            pltpu.SMEM((2 * 8, LANES), jnp.int32),
            dma((CHUNKS,)), dma((CHUNKS,)), dma(()), dma(()), dma(()), dma(()),
            dma((8,)), dma((8,)), dma((8,)), dma((8,)),
            dma((CHUNKS + 1,)), dma((CHUNKS + 1,)), dma((CHUNKS + 1,)), dma((CHUNKS,)), dma((PARTS,)),
            dma((2,)),
        ],
        compiler_params=pltpu.CompilerParams(
            collective_id=0, has_side_effects=True, vmem_limit_bytes=57 * 2**20),
        name="block_sparse_layer",
    )(x, gain.reshape(1, 512), w_own, jnp.transpose(targets), sharp)
    return jnp.dot(attended, wf, preferred_element_type=F32).astype(BF)


def solution(mesh):
    placed = (P(("seq", "head"), None), P(), P(), P(None, None, "head"), P(), P("seq", None))
    return jax.shard_map(
        on_device, mesh=mesh, in_specs=placed, out_specs=P(("seq", "head"), None), check_vma=False
    )
```

```python
import math
import jax
import jax.numpy as jnp
from jax import lax
from jax.experimental import pallas as pl
from jax.experimental.pallas import tpu as pltpu
from jax.sharding import PartitionSpec as P

MESH = pl.DeviceIdType.MESH
BF = jnp.bfloat16
F32 = jnp.float32
GROUPS = 32
PARTS = 8
PAIRS = 4
WIDTH = 64
BLK = 128
KB = 12
KL = 10
FAR = 2
CAP = 6
HALF = 3
RING = 8
ROWS = 8
GROUP_BLOCKS = 64
SUB = 16
CHUNKS = 4
LANES = 128
TOGETHER = 4
FINISH = 4
LOG2E = math.log2(math.e)
EPS = 1e-06


def wait_bytes(ref, sem):
    pltpu.make_async_copy(ref, ref, sem).wait()


def kernel(
    x_ref, gain_ref, w_ref, targets_ref, sharp_ref,
    out_ref,
    x_all, w_all, wk, wv, wq, kp, vp, kf, vf, q_all, num, den,
    xa0, xa1, xa2, xa3, zr0, zr1, zr2, zr3a, zr3b,
    x_in,
    zs, xs, xs3, xr, xr3, listing, req, rq, rqs, tab, tabs,
    xa_ss, xa_rs, rq_ss, rq_rs, rq_ls, tab_ls, w_ss, w_rs, ag_ss, ag_rs, z_ss, z_rs, xr_ss, xr_rs, far_rs, in_ls,
):
    me = lax.axis_index("seq")
    mh = lax.axis_index("head")
    core = lax.rem(mh, 2)
    right = lax.rem(mh + 2, PARTS)
    left = lax.rem(mh + 6, PARTS)
    opp = lax.rem(mh + 4, PARTS)
    sib = mh + 1 - 2 * core
    sib_right = right + 1 - 2 * core
    sib_left = left + 1 - 2 * core
    sib_opp = opp + 1 - 2 * core
    xas = (xa0, xa1, xa2, xa3)
    zrs = (zr0, zr1, zr2, zr3a, zr3b)

    barrier = pltpu.get_barrier_semaphore()
    load_x = pltpu.make_async_copy(x_ref, x_in, in_ls.at[0])
    load_w = pltpu.make_async_copy(w_ref, w_all.at[mh], in_ls.at[1])
    load_x.start()
    load_w.start()

    def greet_seq(d, carry):
        pl.semaphore_signal(barrier, inc=1, device_id={"seq": lax.rem(me + d, GROUPS)}, device_id_type=MESH)
        return carry

    def greet_head(d, carry):
        pl.semaphore_signal(barrier, inc=1, device_id={"head": lax.rem(mh + d, PARTS)}, device_id_type=MESH)
        return carry

    lax.fori_loop(1, GROUPS, greet_seq, 0)
    lax.fori_loop(1, PARTS, greet_head, 0)

    gain = gain_ref[...]

    def norm_block(i, carry):
        rows = x_in[pl.ds(pl.multiple_of(i * BLK, BLK), BLK), :].astype(F32)
        scale = lax.rsqrt(jnp.mean(rows * rows, axis=-1, keepdims=True) + EPS)
        x_all[mh, i] = (rows * scale * gain).astype(BF)
        return carry

    load_x.wait()
    lax.fori_loop(0, ROWS, norm_block, 0)

    pl.semaphore_wait(barrier, GROUPS - 1 + PARTS - 1)

    def send_sub(c):
        def go(d, carry):
            t = lax.rem(mh + d, PARTS)
            pltpu.make_async_remote_copy(
                src_ref=x_all.at[mh, :, pl.ds(pl.multiple_of(t * SUB, SUB), SUB), pl.ds(c * LANES, LANES)],
                dst_ref=xas[c].at[pl.ds(mh * ROWS, ROWS)],
                send_sem=xa_ss.at[c], recv_sem=xa_rs.at[c],
                device_id={"head": t}, device_id_type=MESH,
            ).start()
            return carry

        lax.fori_loop(1, PARTS, go, 0)
        xas[c][pl.ds(mh * ROWS, ROWS)] = x_all[
            mh, :, pl.ds(pl.multiple_of(mh * SUB, SUB), SUB), pl.ds(c * LANES, LANES)]

    send_sub(0)

    listing[...] = jnp.full(listing.shape, -GROUP_BLOCKS, jnp.int32)
    listing[0:KB, 0:GROUP_BLOCKS] = targets_ref[...]
    lane = lax.broadcasted_iota(jnp.int32, (1, LANES), 1)
    none = jnp.zeros((1, LANES), jnp.int32)
    near_count, far_count = none, none
    near_rows = [none] * KL
    owners, withins = [none] * FAR, [none] * FAR
    for j in range(KB):
        target = listing[j:j + 1, :]
        owner = lax.shift_right_arithmetic(target, 6)
        within = target - owner * GROUP_BLOCKS
        is_far = owner != me
        for k in range(KL):
            near_rows[k] = jnp.where(jnp.logical_and(owner == me, near_count == k), within, near_rows[k])
        for k in range(FAR):
            here = jnp.logical_and(is_far, far_count == k)
            owners[k] = jnp.where(here, owner, owners[k])
            withins[k] = jnp.where(here, within, withins[k])
        near_count = near_count + jnp.where(is_far, 0, 1)
        far_count = far_count + jnp.where(is_far, 1, 0)
    group = lax.broadcasted_iota(jnp.int32, (GROUPS, LANES), 0)
    hits = [jnp.where(group == owners[k], 1, 0) for k in range(FAR)]
    both = hits[0] + hits[1]
    counted = both
    wide_lane = lax.broadcasted_iota(jnp.int32, (GROUPS, LANES), 1)
    for step in (1, 2, 4, 8, 16, 32):
        counted = counted + jnp.where(wide_lane >= step, pltpu.roll(counted, step, 1), 0)
    counted = counted - both

    def over_groups(value):
        eight = value[0:8] + value[8:16] + value[16:24] + value[24:32]
        four = eight[0:4] + eight[4:8]
        two = four[0:2] + four[2:4]
        return two[0:1] + two[1:2]

    slots = [over_groups(hits[0] * counted), over_groups(hits[1] * (counted + hits[0]))]
    wanted = jnp.zeros((GROUPS, LANES), jnp.int32)
    for c in range(CAP):
        one = none
        for k in range(FAR):
            one = one + hits[k] * jnp.where(slots[k] == c, withins[k], 0)
        for step in (1, 2, 4, 8, 16, 32, 64):
            one = one + pltpu.roll(one, step, 1)
        wanted = jnp.where(wide_lane == c, one, wanted)
    for o in range(GROUPS):
        req[o] = wanted[o:o + 1, :]
    rq[me] = req[me]

    def send_req(d, carry):
        t = lax.rem(me + d, GROUPS)
        pltpu.make_async_remote_copy(
            src_ref=req.at[t], dst_ref=rq.at[me], send_sem=rq_ss, recv_sem=rq_rs,
            device_id={"seq": t}, device_id_type=MESH,
        ).start()
        return carry

    lax.fori_loop(1, GROUPS, send_req, 0)

    for k in range(KL):
        tab[k:k + 1, :] = near_rows[k]
    for k in range(FAR):
        tab[KL + k:KL + k + 1, :] = owners[k] * CAP + slots[k]
    tab[KB:16, :] = jnp.zeros((16 - KB, LANES), jnp.int32)
    to_tabs = pltpu.make_async_copy(tab, tabs, tab_ls)
    to_tabs.start()

    low = lane < WIDTH
    load_w.wait()

    def ring(buf, ss, rs, half):
        first, second = pl.ds(0, half), pl.ds(half, half)

        def copy(k, view, to):
            return pltpu.make_async_remote_copy(
                src_ref=view, dst_ref=view, send_sem=ss.at[k], recv_sem=rs.at[k],
                device_id={"head": to}, device_id_type=MESH)

        return (
            copy(0, buf.at[mh], right), copy(1, buf.at[mh], left), copy(2, buf.at[mh], sib),
            copy(3, buf.at[left, first], right), copy(4, buf.at[right, second], left),
            copy(5, buf.at[left], sib), copy(6, buf.at[right], sib), copy(7, buf.at[opp], sib),
        )

    w_ring = ring(w_all, w_ss, w_rs, w_all.shape[1] // 2)
    x_ring = ring(x_all, ag_ss, ag_rs, ROWS // 2)

    for k in (0, 1, 2):
        w_ring[k].start()
    for c in range(1, CHUNKS):
        send_sub(c)
    for k in (0, 1, 2):
        x_ring[k].start()

    wait_bytes(rq.at[pl.ds(0, GROUPS - 1)], rq_rs)
    to_smem = pltpu.make_async_copy(rq, rqs, rq_ls)
    to_smem.start()
    to_smem.wait()

    def send_slots(c, k, t, first, count):
        pltpu.make_async_remote_copy(
            src_ref=zs.at[c, pl.ds(first + t * count, count)], dst_ref=zrs[k].at[pl.ds(me * count, count)],
            send_sem=z_ss.at[k], recv_sem=z_rs.at[k],
            device_id={"seq": t}, device_id_type=MESH,
        ).start()

    def send_groups(c):
        wait_bytes(xas[c].at[pl.ds(0, GROUP_BLOCKS - ROWS)], xa_rs.at[c])

        def one(dy, dz):
            t = lax.rem(me // RING + dy, GROUPS // RING) * RING + lax.rem(me + dz, RING)
            if c < CHUNKS - 1:
                for s in range(CAP):
                    zs[c, t * CAP + s] = xas[c][rqs[t, 0, s]]
                send_slots(c, c, t, 0, CAP)
                return
            for s in range(HALF):
                a = xas[c][rqs[t, 0, 2 * s]].astype(F32)
                b = xas[c][rqs[t, 0, 2 * s + 1]].astype(F32)
                zs[c, t * HALF + s] = jnp.concatenate([a[0:8], b[0:8]], axis=0).astype(BF)
                zs[c, GROUPS * HALF + t * HALF + s] = jnp.concatenate([a[8:16], b[8:16]], axis=0).astype(BF)
            send_slots(c, c, t, 0, HALF)

        def go(i, carry):
            dz = jnp.where(i % 2 == 0, 1 + i // 2, RING - 1 - i // 2)
            for dy in (0, 1, 3, 2):
                one(dy, dz)
            return carry

        lax.fori_loop(0, RING - 1, go, 0)
        for dy in (1, 3, 2):
            one(dy, 0)

    def send_rest():
        def one(dy, dz):
            t = lax.rem(me // RING + dy, GROUPS // RING) * RING + lax.rem(me + dz, RING)
            send_slots(CHUNKS - 1, CHUNKS, t, GROUPS * HALF, HALF)

        def go(i, carry):
            dz = jnp.where(i % 2 == 0, 1 + i // 2, RING - 1 - i // 2)
            for dy in (0, 1, 3, 2):
                one(dy, dz)
            return carry

        lax.fori_loop(0, RING - 1, go, 0)
        for dy in (1, 3, 2):
            one(dy, 0)

    send_groups(0)
    w_ring[0].wait_recv()
    w_ring[1].wait_recv()
    for k in (3, 4, 5, 6):
        w_ring[k].start()
    send_groups(1)
    w_ring[3].wait_recv()
    w_ring[4].wait_recv()
    w_ring[7].start()
    send_groups(2)
    send_groups(3)
    send_rest()
    for k in (2, 5, 6, 7):
        w_ring[k].wait_recv()
    to_tabs.wait()

    for k, ref in enumerate((wq, wk, wv)):
        for t in range(2):
            ref[t] = jnp.transpose(
                jnp.concatenate([w_all[4 * t + n, k * WIDTH:(k + 1) * WIDTH] for n in range(4)], axis=0), (1, 0))

    row2 = lax.broadcasted_iota(jnp.int32, (2 * LANES, 2 * LANES), 0)
    col2 = lax.broadcasted_iota(jnp.int32, (2 * LANES, 2 * LANES), 1)
    spread = jnp.where(row2 // WIDTH == col2 // WIDTH, 1.0 / WIDTH, 0.0).astype(BF)

    def unit_rows(rows, weights):
        wide = jnp.dot(rows, weights, preferred_element_type=F32).astype(BF).astype(F32)
        mean = jnp.dot((wide * wide).astype(BF), spread, preferred_element_type=F32)
        return (wide * lax.rsqrt(mean + EPS)).astype(BF)

    def plain_rows(rows, weights):
        return jnp.dot(rows, weights, preferred_element_type=F32).astype(BF)

    def project(s):
        def go(i, carry):
            rows = x_all[s, pl.ds(TOGETHER * i, TOGETHER)].reshape(TOGETHER * BLK, 512)
            for t in range(2):
                for ref, both in ((kp, unit_rows(rows, wk[t])), (vp, plain_rows(rows, wv[t]))):
                    for n in range(2):
                        for m in range(TOGETHER):
                            ref[s * ROWS + TOGETHER * i + m, 2 * t + n] = both[
                                m * BLK:(m + 1) * BLK, n * LANES:(n + 1) * LANES]
            return carry

        lax.fori_loop(0, ROWS // TOGETHER, go, 0)

    def project_queries():
        def go(i, carry):
            rows = x_all[mh, pl.ds(TOGETHER * i, TOGETHER)].reshape(TOGETHER * BLK, 512)
            for t in range(2):
                both = unit_rows(rows, wq[t])
                for n in range(2):
                    for m in range(TOGETHER):
                        one = both[m * BLK:(m + 1) * BLK, n * LANES:(n + 1) * LANES]
                        none = jnp.zeros_like(one)
                        q_all[TOGETHER * i + m, 2 * t + n, 0:BLK] = jnp.where(low, one, none)
                        q_all[TOGETHER * i + m, 2 * t + n, BLK:2 * BLK] = jnp.where(low, none, one)
            return carry

        lax.fori_loop(0, ROWS // TOGETHER, go, 0)

    def score(q, keys):
        return lax.dot_general(q, keys, (((1,), (1,)), ((), ())), preferred_element_type=F32)

    def blend(scores, values, p):
        weights = []
        for n in range(2):
            sharp = sharp_ref[2 * p + n]
            weights.append(jnp.exp2(
                scores[n * BLK:(n + 1) * BLK] * (sharp * (LOG2E / WIDTH)) - sharp * LOG2E).astype(BF))
        values = jnp.concatenate([values, jnp.ones_like(values)], axis=1)
        return jnp.dot(jnp.concatenate(weights, axis=0), values, preferred_element_type=F32)

    def parted(both):
        return (jnp.where(low, both[0:BLK, 0:LANES], both[BLK:2 * BLK, 0:LANES]),
                jnp.where(low, both[0:BLK, LANES:2 * LANES], both[BLK:2 * BLK, LANES:2 * LANES]))

    def near(first, last):
        def go(b, carry):
            listed = [tabs[j, mh * ROWS + b] for j in range(KL)]
            scores = [
                score(q_all[b, p], jnp.concatenate([kp[i, p] for i in listed], axis=0)) for p in range(PAIRS)]
            for p in range(PAIRS):
                both = blend(scores[p], jnp.concatenate([vp[i, p] for i in listed], axis=0), p)
                num[b, p], den[b, p] = parted(both)
            return carry

        lax.fori_loop(first, last, go, 0)

    def pass_on(k):
        c, half = (k, 0) if k < CHUNKS else (CHUNKS - 1, 1)
        halved = c == CHUNKS - 1
        count = HALF if halved else CAP
        wait_bytes(zrs[k].at[pl.ds(0, (GROUPS - 1) * count)], z_rs.at[k])

        def part(t, b, j):
            place = tabs[KL + j, t * ROWS + b]
            both = zrs[k][lax.shift_right_arithmetic(place, 1)].astype(F32)
            upper = jnp.full((8, LANES), place & 1, jnp.int32) == 0
            return jnp.where(upper, both[0:8], both[8:16])

        def go(i, carry):
            t = lax.rem(mh + jnp.where(i % 2 == 0, 4 + i // 2, 3 - i // 2), PARTS)
            if halved:
                for b in range(ROWS):
                    xs3[half, t, b] = jnp.concatenate([part(t, b, 0), part(t, b, 1)], axis=0).astype(BF)
                src, dst = xs3.at[half, t], xr3.at[half, mh]
            else:
                for e in range(ROWS * FAR):
                    xs[c, t, e] = zrs[c][tabs[KL + e % FAR, t * ROWS + e // FAR]]
                src, dst = xs.at[c, t], xr.at[mh, :, :, pl.ds(c * LANES, LANES)]

            @pl.when(i < PARTS - 1)
            def _():
                pltpu.make_async_remote_copy(
                    src_ref=src, dst_ref=dst,
                    send_sem=xr_ss.at[k], recv_sem=xr_rs.at[k] if k < CHUNKS else far_rs.at[mh],
                    device_id={"head": t}, device_id_type=MESH,
                ).start()

            return carry

        lax.fori_loop(0, PARTS, go, 0)
        if halved:
            xr3[half, mh] = xs3[half, mh]
        else:
            xr[mh, :, :, pl.ds(c * LANES, LANES)] = xs[c, mh]

    project(mh)
    x_ring[0].wait_recv()
    x_ring[1].wait_recv()
    for k in (3, 4, 5, 6):
        x_ring[k].start()
    x_ring[2].wait_recv()
    project(sib)
    project_queries()
    project(left)
    project(right)
    pass_on(0)
    x_ring[3].wait_recv()
    x_ring[4].wait_recv()
    x_ring[7].start()
    project(opp)
    x_ring[5].wait_recv()
    project(sib_left)
    x_ring[6].wait_recv()
    project(sib_right)
    pass_on(1)
    x_ring[7].wait_recv()
    project(sib_opp)
    pass_on(2)
    near(0, 4)
    pass_on(3)
    near(4, 6)
    pass_on(4)
    near(6, ROWS)
    for c in range(CHUNKS - 1):
        wait_bytes(xs.at[c, pl.ds(0, PARTS - 1)], xr_rs.at[c])
    wait_bytes(xs3.at[0, pl.ds(0, PARTS - 1)], xr_rs.at[CHUNKS - 1])

    sources = (mh, sib, left, right, sib_left, sib_right, opp, sib_opp)

    def project_far(k):
        count = ROWS * FAR * SUB
        for s in sources[k:k + 2]:
            if s is not mh:
                wait_bytes(xs3.at[1, 0], far_rs.at[s])
            first, second = xr3[0, s].astype(F32), xr3[1, s].astype(F32)
            rows = [jnp.concatenate([first[:, r:r + 8], second[:, r:r + 8]], axis=1) for r in (0, 8)]
            xr[s, :, :, pl.ds((CHUNKS - 1) * LANES, LANES)] = jnp.stack(rows, axis=1).reshape(
                ROWS * FAR, SUB, LANES).astype(BF)
        rows = jnp.concatenate([xr[s].reshape(count, 512) for s in sources[k:k + 2]], axis=0)
        for t in range(2):
            for ref, both in ((kf, unit_rows(rows, wk[t])), (vf, plain_rows(rows, wv[t]))):
                for n in range(2):
                    for m in range(2):
                        ref[2 * t + n, :, (k + m) * SUB:(k + m + 1) * SUB, :] = both[
                            m * count:(m + 1) * count, n * LANES:(n + 1) * LANES].reshape(ROWS * FAR, SUB, LANES)

    def far_keys(ref, b, p):
        return ref[p, pl.ds(FAR * b, FAR)].reshape(FAR * BLK, LANES)

    def finish(i, carry):
        units = [(FINISH * i + m, p) for m in range(FINISH) for p in range(PAIRS)]
        scores = [score(q_all[b, p], far_keys(kf, b, p)) for b, p in units]
        for (b, p), one in zip(units, scores):
            top, bottom = parted(blend(one, far_keys(vf, b, p), p))
            out_ref[pl.ds(pl.multiple_of(b * BLK, BLK), BLK), p * LANES:(p + 1) * LANES] = (
                (num[b, p] + top) / (den[b, p] + bottom)).astype(BF)
        return carry

    for k in range(0, PARTS, 2):
        project_far(k)
    lax.fori_loop(0, ROWS // FINISH, finish, 0)

    wait_bytes(rq.at[pl.ds(0, GROUPS - 1)], rq_ss)
    for c in range(CHUNKS):
        wait_bytes(xas[c].at[pl.ds(0, GROUP_BLOCKS - ROWS)], xa_ss.at[c])
        if c < CHUNKS - 1:
            wait_bytes(zs.at[c, pl.ds(0, (GROUPS - 1) * CAP)], z_ss.at[c])
            wait_bytes(xs.at[c, pl.ds(0, PARTS - 1)], xr_ss.at[c])
    for k in (CHUNKS - 1, CHUNKS):
        wait_bytes(zs.at[0, pl.ds(0, (GROUPS - 1) * HALF)], z_ss.at[k])
        wait_bytes(xs3.at[0, pl.ds(0, PARTS - 1)], xr_ss.at[k])
    for k in range(8):
        w_ring[k].wait_send()
        x_ring[k].wait_send()


def on_device(x, gain, sharp, w3, wf, targets):
    w_own = jnp.transpose(w3, (1, 2, 0)).reshape(3 * WIDTH, 512)
    vmem = pl.BlockSpec(memory_space=pltpu.VMEM)
    smem = pl.BlockSpec(memory_space=pltpu.SMEM)
    hbm = pl.BlockSpec(memory_space=pl.ANY)
    dma = pltpu.SemaphoreType.DMA
    sub = pltpu.VMEM((GROUP_BLOCKS, SUB, LANES), BF)
    landed = pltpu.VMEM((GROUPS * CAP, SUB, LANES), BF)
    half_landed = pltpu.VMEM((GROUPS * HALF, SUB, LANES), BF)
    blocks = pltpu.VMEM((GROUP_BLOCKS, PAIRS, BLK, LANES), BF)
    far_blocks = pltpu.VMEM((PAIRS, ROWS * FAR, BLK, LANES), BF)
    sums = pltpu.VMEM((ROWS, PAIRS, BLK, LANES), F32)
    weights = pltpu.VMEM((2, 512, 2 * LANES), BF)
    attended = pl.pallas_call(
        kernel,
        out_shape=pltpu.VMEM(x.shape, BF),
        in_specs=[hbm, vmem, hbm, vmem, smem],
        out_specs=vmem,
        scratch_shapes=[
            pltpu.VMEM((PARTS, ROWS, BLK, 512), BF),
            pltpu.VMEM((PARTS, 3 * WIDTH, 512), BF),
            weights, weights, weights,
            blocks, blocks, far_blocks, far_blocks,
            pltpu.VMEM((ROWS, PAIRS, 2 * BLK, LANES), BF),
            sums, sums,
            sub, sub, sub, sub, landed, landed, landed, half_landed, half_landed,
            pltpu.VMEM(x.shape, BF),
            pltpu.VMEM((CHUNKS, GROUPS * CAP, SUB, LANES), BF),
            pltpu.VMEM((CHUNKS - 1, PARTS, ROWS * FAR, SUB, LANES), BF),
            pltpu.VMEM((2, PARTS, ROWS, SUB, LANES), BF),
            pltpu.VMEM((PARTS, ROWS * FAR, SUB, 512), BF),
            pltpu.VMEM((2, PARTS, ROWS, SUB, LANES), BF),
            pltpu.VMEM((2 * 8, LANES), jnp.int32),
            pltpu.VMEM((GROUPS, 1, LANES), jnp.int32),
            pltpu.VMEM((GROUPS, 1, LANES), jnp.int32),
            pltpu.SMEM((GROUPS, 1, LANES), jnp.int32),
            pltpu.VMEM((2 * 8, LANES), jnp.int32),
            pltpu.SMEM((2 * 8, LANES), jnp.int32),
            dma((CHUNKS,)), dma((CHUNKS,)), dma(()), dma(()), dma(()), dma(()),
            dma((8,)), dma((8,)), dma((8,)), dma((8,)),
            dma((CHUNKS + 1,)), dma((CHUNKS + 1,)), dma((CHUNKS + 1,)), dma((CHUNKS,)), dma((PARTS,)),
            dma((2,)),
        ],
        compiler_params=pltpu.CompilerParams(
            collective_id=0, has_side_effects=True, vmem_limit_bytes=57 * 2**20),
        name="block_sparse_layer",
    )(x, gain.reshape(1, 512), w_own, jnp.transpose(targets), sharp)
    return jnp.dot(attended, wf, preferred_element_type=F32).astype(BF)


def solution(mesh):
    placed = (P(("seq", "head"), None), P(), P(), P(None, None, "head"), P(), P("seq", None))
    return jax.shard_map(
        on_device, mesh=mesh, in_specs=placed, out_specs=P(("seq", "head"), None), check_vma=False
    )
```

```python
import math
import jax
import jax.numpy as jnp
from jax import lax
from jax.experimental import pallas as pl
from jax.experimental.pallas import tpu as pltpu
from jax.sharding import PartitionSpec as P

MESH = pl.DeviceIdType.MESH
BF = jnp.bfloat16
F32 = jnp.float32
GROUPS = 32
PARTS = 8
PAIRS = 4
WIDTH = 64
BLK = 128
KB = 12
KL = 10
FAR = 2
CAP = 6
HALF = 3
RING = 8
ROWS = 8
GROUP_BLOCKS = 64
SUB = 16
CHUNKS = 4
LANES = 128
TOGETHER = 4
FINISH = 4
LOG2E = math.log2(math.e)
EPS = 1e-06


def wait_bytes(ref, sem):
    pltpu.make_async_copy(ref, ref, sem).wait()


def kernel(
    x_ref, gain_ref, w_ref, targets_ref, sharp_ref,
    out_ref,
    x_all, w_all, wk, wv, wq, kp, vp, kf, vf, q_all, num, den,
    xa0, xa1, xa2, xa3, zr0, zr1, zr2, zr3a, zr3b,
    x_in,
    zs, xs, xs3, xr, xr3, listing, req, rq, rqs, tab, tabs,
    xa_ss, xa_rs, rq_ss, rq_rs, rq_ls, tab_ls, w_ss, w_rs, ag_ss, ag_rs, z_ss, z_rs, xr_ss, xr_rs, far_rs, in_ls,
):
    me = lax.axis_index("seq")
    mh = lax.axis_index("head")
    core = lax.rem(mh, 2)
    right = lax.rem(mh + 2, PARTS)
    left = lax.rem(mh + 6, PARTS)
    opp = lax.rem(mh + 4, PARTS)
    sib = mh + 1 - 2 * core
    sib_right = right + 1 - 2 * core
    sib_left = left + 1 - 2 * core
    sib_opp = opp + 1 - 2 * core
    xas = (xa0, xa1, xa2, xa3)
    zrs = (zr0, zr1, zr2, zr3a, zr3b)

    barrier = pltpu.get_barrier_semaphore()
    load_x = pltpu.make_async_copy(x_ref, x_in, in_ls.at[0])
    load_w = pltpu.make_async_copy(w_ref, w_all.at[mh], in_ls.at[1])
    load_x.start()
    load_w.start()

    def greet_seq(d, carry):
        pl.semaphore_signal(barrier, inc=1, device_id={"seq": lax.rem(me + d, GROUPS)}, device_id_type=MESH)
        return carry

    def greet_head(d, carry):
        pl.semaphore_signal(barrier, inc=1, device_id={"head": lax.rem(mh + d, PARTS)}, device_id_type=MESH)
        return carry

    lax.fori_loop(1, GROUPS, greet_seq, 0)
    lax.fori_loop(1, PARTS, greet_head, 0)

    gain = gain_ref[...]

    def norm_block(i, carry):
        rows = x_in[pl.ds(pl.multiple_of(i * BLK, BLK), BLK), :].astype(F32)
        scale = lax.rsqrt(jnp.mean(rows * rows, axis=-1, keepdims=True) + EPS)
        x_all[mh, i] = (rows * scale * gain).astype(BF)
        return carry

    load_x.wait()
    lax.fori_loop(0, ROWS, norm_block, 0)

    pl.semaphore_wait(barrier, GROUPS - 1 + PARTS - 1)

    def send_sub(c):
        def go(d, carry):
            t = lax.rem(mh + d, PARTS)
            pltpu.make_async_remote_copy(
                src_ref=x_all.at[mh, :, pl.ds(pl.multiple_of(t * SUB, SUB), SUB), pl.ds(c * LANES, LANES)],
                dst_ref=xas[c].at[pl.ds(mh * ROWS, ROWS)],
                send_sem=xa_ss.at[c], recv_sem=xa_rs.at[c],
                device_id={"head": t}, device_id_type=MESH,
            ).start()
            return carry

        lax.fori_loop(1, PARTS, go, 0)
        xas[c][pl.ds(mh * ROWS, ROWS)] = x_all[
            mh, :, pl.ds(pl.multiple_of(mh * SUB, SUB), SUB), pl.ds(c * LANES, LANES)]

    send_sub(0)

    listing[...] = jnp.full(listing.shape, -GROUP_BLOCKS, jnp.int32)
    listing[0:KB, 0:GROUP_BLOCKS] = targets_ref[...]
    lane = lax.broadcasted_iota(jnp.int32, (1, LANES), 1)
    none = jnp.zeros((1, LANES), jnp.int32)
    near_count, far_count = none, none
    near_rows = [none] * KL
    owners, withins = [none] * FAR, [none] * FAR
    for j in range(KB):
        target = listing[j:j + 1, :]
        owner = lax.shift_right_arithmetic(target, 6)
        within = target - owner * GROUP_BLOCKS
        is_far = owner != me
        for k in range(KL):
            near_rows[k] = jnp.where(jnp.logical_and(owner == me, near_count == k), within, near_rows[k])
        for k in range(FAR):
            here = jnp.logical_and(is_far, far_count == k)
            owners[k] = jnp.where(here, owner, owners[k])
            withins[k] = jnp.where(here, within, withins[k])
        near_count = near_count + jnp.where(is_far, 0, 1)
        far_count = far_count + jnp.where(is_far, 1, 0)
    group = lax.broadcasted_iota(jnp.int32, (GROUPS, LANES), 0)
    hits = [jnp.where(group == owners[k], 1, 0) for k in range(FAR)]
    both = hits[0] + hits[1]
    counted = both
    wide_lane = lax.broadcasted_iota(jnp.int32, (GROUPS, LANES), 1)
    for step in (1, 2, 4, 8, 16, 32):
        counted = counted + jnp.where(wide_lane >= step, pltpu.roll(counted, step, 1), 0)
    counted = counted - both

    def over_groups(value):
        eight = value[0:8] + value[8:16] + value[16:24] + value[24:32]
        four = eight[0:4] + eight[4:8]
        two = four[0:2] + four[2:4]
        return two[0:1] + two[1:2]

    slots = [over_groups(hits[0] * counted), over_groups(hits[1] * (counted + hits[0]))]
    wanted = jnp.zeros((GROUPS, LANES), jnp.int32)
    for c in range(CAP):
        one = none
        for k in range(FAR):
            one = one + hits[k] * jnp.where(slots[k] == c, withins[k], 0)
        for step in (1, 2, 4, 8, 16, 32, 64):
            one = one + pltpu.roll(one, step, 1)
        wanted = jnp.where(wide_lane == c, one, wanted)
    for o in range(GROUPS):
        req[o] = wanted[o:o + 1, :]
    rq[me] = req[me]

    def send_req(d, carry):
        t = lax.rem(me + d, GROUPS)
        pltpu.make_async_remote_copy(
            src_ref=req.at[t], dst_ref=rq.at[me], send_sem=rq_ss, recv_sem=rq_rs,
            device_id={"seq": t}, device_id_type=MESH,
        ).start()
        return carry

    lax.fori_loop(1, GROUPS, send_req, 0)

    for k in range(KL):
        tab[k:k + 1, :] = near_rows[k]
    for k in range(FAR):
        tab[KL + k:KL + k + 1, :] = owners[k] * CAP + slots[k]
    tab[KB:16, :] = jnp.zeros((16 - KB, LANES), jnp.int32)
    to_tabs = pltpu.make_async_copy(tab, tabs, tab_ls)
    to_tabs.start()

    low = lane < WIDTH
    load_w.wait()

    def ring(buf, ss, rs, half):
        first, second = pl.ds(0, half), pl.ds(half, half)

        def copy(k, view, to):
            return pltpu.make_async_remote_copy(
                src_ref=view, dst_ref=view, send_sem=ss.at[k], recv_sem=rs.at[k],
                device_id={"head": to}, device_id_type=MESH)

        return (
            copy(0, buf.at[mh], right), copy(1, buf.at[mh], left), copy(2, buf.at[mh], sib),
            copy(3, buf.at[left, first], right), copy(4, buf.at[right, second], left),
            copy(5, buf.at[left], sib), copy(6, buf.at[right], sib), copy(7, buf.at[opp], sib),
        )

    w_ring = ring(w_all, w_ss, w_rs, w_all.shape[1] // 2)
    x_ring = ring(x_all, ag_ss, ag_rs, ROWS // 2)

    for k in (0, 1, 2):
        w_ring[k].start()
    for c in range(1, CHUNKS):
        send_sub(c)
    for k in (0, 1, 2):
        x_ring[k].start()

    wait_bytes(rq.at[pl.ds(0, GROUPS - 1)], rq_rs)
    to_smem = pltpu.make_async_copy(rq, rqs, rq_ls)
    to_smem.start()
    to_smem.wait()

    def send_slots(c, k, t, first, count):
        pltpu.make_async_remote_copy(
            src_ref=zs.at[c, pl.ds(first + t * count, count)], dst_ref=zrs[k].at[pl.ds(me * count, count)],
            send_sem=z_ss.at[k], recv_sem=z_rs.at[k],
            device_id={"seq": t}, device_id_type=MESH,
        ).start()

    def send_groups(c):
        wait_bytes(xas[c].at[pl.ds(0, GROUP_BLOCKS - ROWS)], xa_rs.at[c])

        def one(dy, dz):
            t = lax.rem(me // RING + dy, GROUPS // RING) * RING + lax.rem(me + dz, RING)
            if c < CHUNKS - 1:
                for s in range(CAP):
                    zs[c, t * CAP + s] = xas[c][rqs[t, 0, s]]
                send_slots(c, c, t, 0, CAP)
                return
            for s in range(HALF):
                a = xas[c][rqs[t, 0, 2 * s]].astype(F32)
                b = xas[c][rqs[t, 0, 2 * s + 1]].astype(F32)
                zs[c, t * HALF + s] = jnp.concatenate([a[0:8], b[0:8]], axis=0).astype(BF)
                zs[c, GROUPS * HALF + t * HALF + s] = jnp.concatenate([a[8:16], b[8:16]], axis=0).astype(BF)
            send_slots(c, c, t, 0, HALF)

        def go(i, carry):
            dz = jnp.where(i % 2 == 0, 1 + i // 2, RING - 1 - i // 2)
            for dy in (0, 1, 3, 2):
                one(dy, dz)
            return carry

        lax.fori_loop(0, RING - 1, go, 0)
        for dy in (1, 3, 2):
            one(dy, 0)

    def send_rest():
        def one(dy, dz):
            t = lax.rem(me // RING + dy, GROUPS // RING) * RING + lax.rem(me + dz, RING)
            send_slots(CHUNKS - 1, CHUNKS, t, GROUPS * HALF, HALF)

        def go(i, carry):
            dz = jnp.where(i % 2 == 0, RING // 2 + i // 2, RING // 2 - 1 - i // 2)
            for dy in (0, 1, 3, 2):
                one(dy, dz)
            return carry

        lax.fori_loop(0, RING - 1, go, 0)
        for dy in (1, 3, 2):
            one(dy, 0)

    send_groups(0)
    w_ring[0].wait_recv()
    w_ring[1].wait_recv()
    for k in (3, 4, 5, 6):
        w_ring[k].start()
    send_groups(1)
    w_ring[3].wait_recv()
    w_ring[4].wait_recv()
    w_ring[7].start()
    send_groups(2)
    send_groups(3)
    send_rest()
    for k in (2, 5, 6, 7):
        w_ring[k].wait_recv()
    to_tabs.wait()

    for k, ref in enumerate((wq, wk, wv)):
        for t in range(2):
            ref[t] = jnp.transpose(
                jnp.concatenate([w_all[4 * t + n, k * WIDTH:(k + 1) * WIDTH] for n in range(4)], axis=0), (1, 0))

    row2 = lax.broadcasted_iota(jnp.int32, (2 * LANES, 2 * LANES), 0)
    col2 = lax.broadcasted_iota(jnp.int32, (2 * LANES, 2 * LANES), 1)
    spread = jnp.where(row2 // WIDTH == col2 // WIDTH, 1.0 / WIDTH, 0.0).astype(BF)

    def unit_rows(rows, weights):
        wide = jnp.dot(rows, weights, preferred_element_type=F32).astype(BF).astype(F32)
        mean = jnp.dot((wide * wide).astype(BF), spread, preferred_element_type=F32)
        return (wide * lax.rsqrt(mean + EPS)).astype(BF)

    def plain_rows(rows, weights):
        return jnp.dot(rows, weights, preferred_element_type=F32).astype(BF)

    def project(s):
        def go(i, carry):
            rows = x_all[s, pl.ds(TOGETHER * i, TOGETHER)].reshape(TOGETHER * BLK, 512)
            for t in range(2):
                for ref, both in ((kp, unit_rows(rows, wk[t])), (vp, plain_rows(rows, wv[t]))):
                    for n in range(2):
                        for m in range(TOGETHER):
                            ref[s * ROWS + TOGETHER * i + m, 2 * t + n] = both[
                                m * BLK:(m + 1) * BLK, n * LANES:(n + 1) * LANES]
            return carry

        lax.fori_loop(0, ROWS // TOGETHER, go, 0)

    def project_queries():
        def go(i, carry):
            rows = x_all[mh, pl.ds(TOGETHER * i, TOGETHER)].reshape(TOGETHER * BLK, 512)
            for t in range(2):
                both = unit_rows(rows, wq[t])
                for n in range(2):
                    for m in range(TOGETHER):
                        one = both[m * BLK:(m + 1) * BLK, n * LANES:(n + 1) * LANES]
                        none = jnp.zeros_like(one)
                        q_all[TOGETHER * i + m, 2 * t + n, 0:BLK] = jnp.where(low, one, none)
                        q_all[TOGETHER * i + m, 2 * t + n, BLK:2 * BLK] = jnp.where(low, none, one)
            return carry

        lax.fori_loop(0, ROWS // TOGETHER, go, 0)

    def score(q, keys):
        return lax.dot_general(q, keys, (((1,), (1,)), ((), ())), preferred_element_type=F32)

    def blend(scores, values, p):
        weights = []
        for n in range(2):
            sharp = sharp_ref[2 * p + n]
            weights.append(jnp.exp2(
                scores[n * BLK:(n + 1) * BLK] * (sharp * (LOG2E / WIDTH)) - sharp * LOG2E).astype(BF))
        values = jnp.concatenate([values, jnp.ones_like(values)], axis=1)
        return jnp.dot(jnp.concatenate(weights, axis=0), values, preferred_element_type=F32)

    def parted(both):
        return (jnp.where(low, both[0:BLK, 0:LANES], both[BLK:2 * BLK, 0:LANES]),
                jnp.where(low, both[0:BLK, LANES:2 * LANES], both[BLK:2 * BLK, LANES:2 * LANES]))

    def near(first, last):
        def go(b, carry):
            listed = [tabs[j, mh * ROWS + b] for j in range(KL)]
            scores = [
                score(q_all[b, p], jnp.concatenate([kp[i, p] for i in listed], axis=0)) for p in range(PAIRS)]
            for p in range(PAIRS):
                both = blend(scores[p], jnp.concatenate([vp[i, p] for i in listed], axis=0), p)
                num[b, p], den[b, p] = parted(both)
            return carry

        lax.fori_loop(first, last, go, 0)

    def pass_on(k):
        c, half = (k, 0) if k < CHUNKS else (CHUNKS - 1, 1)
        halved = c == CHUNKS - 1
        count = HALF if halved else CAP
        wait_bytes(zrs[k].at[pl.ds(0, (GROUPS - 1) * count)], z_rs.at[k])

        def part(t, b, j):
            place = tabs[KL + j, t * ROWS + b]
            both = zrs[k][lax.shift_right_arithmetic(place, 1)].astype(F32)
            upper = jnp.full((8, LANES), place & 1, jnp.int32) == 0
            return jnp.where(upper, both[0:8], both[8:16])

        def go(i, carry):
            t = lax.rem(mh + jnp.where(i % 2 == 0, 4 + i // 2, 3 - i // 2), PARTS)
            if halved:
                for b in range(ROWS):
                    xs3[half, t, b] = jnp.concatenate([part(t, b, 0), part(t, b, 1)], axis=0).astype(BF)
                src, dst = xs3.at[half, t], xr3.at[half, mh]
            else:
                for e in range(ROWS * FAR):
                    xs[c, t, e] = zrs[c][tabs[KL + e % FAR, t * ROWS + e // FAR]]
                src, dst = xs.at[c, t], xr.at[mh, :, :, pl.ds(c * LANES, LANES)]

            @pl.when(i < PARTS - 1)
            def _():
                pltpu.make_async_remote_copy(
                    src_ref=src, dst_ref=dst,
                    send_sem=xr_ss.at[k], recv_sem=xr_rs.at[k] if k < CHUNKS else far_rs.at[mh],
                    device_id={"head": t}, device_id_type=MESH,
                ).start()

            return carry

        lax.fori_loop(0, PARTS, go, 0)
        if halved:
            xr3[half, mh] = xs3[half, mh]
        else:
            xr[mh, :, :, pl.ds(c * LANES, LANES)] = xs[c, mh]

    project(mh)
    x_ring[0].wait_recv()
    x_ring[1].wait_recv()
    for k in (3, 4, 5, 6):
        x_ring[k].start()
    x_ring[2].wait_recv()
    project(sib)
    project_queries()
    project(left)
    project(right)
    pass_on(0)
    x_ring[3].wait_recv()
    x_ring[4].wait_recv()
    x_ring[7].start()
    project(opp)
    x_ring[5].wait_recv()
    project(sib_left)
    x_ring[6].wait_recv()
    project(sib_right)
    pass_on(1)
    x_ring[7].wait_recv()
    project(sib_opp)
    pass_on(2)
    near(0, 4)
    pass_on(3)
    near(4, 6)
    pass_on(4)
    near(6, ROWS)
    for c in range(CHUNKS - 1):
        wait_bytes(xs.at[c, pl.ds(0, PARTS - 1)], xr_rs.at[c])
    wait_bytes(xs3.at[0, pl.ds(0, PARTS - 1)], xr_rs.at[CHUNKS - 1])

    sources = (mh, sib, left, right, sib_left, sib_right, opp, sib_opp)

    def project_far(k):
        count = ROWS * FAR * SUB
        for s in sources[k:k + 2]:
            if s is not mh:
                wait_bytes(xs3.at[1, 0], far_rs.at[s])
            first, second = xr3[0, s].astype(F32), xr3[1, s].astype(F32)
            rows = [jnp.concatenate([first[:, r:r + 8], second[:, r:r + 8]], axis=1) for r in (0, 8)]
            xr[s, :, :, pl.ds((CHUNKS - 1) * LANES, LANES)] = jnp.stack(rows, axis=1).reshape(
                ROWS * FAR, SUB, LANES).astype(BF)
        rows = jnp.concatenate([xr[s].reshape(count, 512) for s in sources[k:k + 2]], axis=0)
        for t in range(2):
            for ref, both in ((kf, unit_rows(rows, wk[t])), (vf, plain_rows(rows, wv[t]))):
                for n in range(2):
                    for m in range(2):
                        ref[2 * t + n, :, (k + m) * SUB:(k + m + 1) * SUB, :] = both[
                            m * count:(m + 1) * count, n * LANES:(n + 1) * LANES].reshape(ROWS * FAR, SUB, LANES)

    def far_keys(ref, b, p):
        return ref[p, pl.ds(FAR * b, FAR)].reshape(FAR * BLK, LANES)

    def finish(i, carry):
        units = [(FINISH * i + m, p) for m in range(FINISH) for p in range(PAIRS)]
        scores = [score(q_all[b, p], far_keys(kf, b, p)) for b, p in units]
        for (b, p), one in zip(units, scores):
            top, bottom = parted(blend(one, far_keys(vf, b, p), p))
            out_ref[pl.ds(pl.multiple_of(b * BLK, BLK), BLK), p * LANES:(p + 1) * LANES] = (
                (num[b, p] + top) / (den[b, p] + bottom)).astype(BF)
        return carry

    for k in range(0, PARTS, 2):
        project_far(k)
    lax.fori_loop(0, ROWS // FINISH, finish, 0)

    wait_bytes(rq.at[pl.ds(0, GROUPS - 1)], rq_ss)
    for c in range(CHUNKS):
        wait_bytes(xas[c].at[pl.ds(0, GROUP_BLOCKS - ROWS)], xa_ss.at[c])
        if c < CHUNKS - 1:
            wait_bytes(zs.at[c, pl.ds(0, (GROUPS - 1) * CAP)], z_ss.at[c])
            wait_bytes(xs.at[c, pl.ds(0, PARTS - 1)], xr_ss.at[c])
    for k in (CHUNKS - 1, CHUNKS):
        wait_bytes(zs.at[0, pl.ds(0, (GROUPS - 1) * HALF)], z_ss.at[k])
        wait_bytes(xs3.at[0, pl.ds(0, PARTS - 1)], xr_ss.at[k])
    for k in range(8):
        w_ring[k].wait_send()
        x_ring[k].wait_send()


def on_device(x, gain, sharp, w3, wf, targets):
    w_own = jnp.transpose(w3, (1, 2, 0)).reshape(3 * WIDTH, 512)
    vmem = pl.BlockSpec(memory_space=pltpu.VMEM)
    smem = pl.BlockSpec(memory_space=pltpu.SMEM)
    hbm = pl.BlockSpec(memory_space=pl.ANY)
    dma = pltpu.SemaphoreType.DMA
    sub = pltpu.VMEM((GROUP_BLOCKS, SUB, LANES), BF)
    landed = pltpu.VMEM((GROUPS * CAP, SUB, LANES), BF)
    half_landed = pltpu.VMEM((GROUPS * HALF, SUB, LANES), BF)
    blocks = pltpu.VMEM((GROUP_BLOCKS, PAIRS, BLK, LANES), BF)
    far_blocks = pltpu.VMEM((PAIRS, ROWS * FAR, BLK, LANES), BF)
    sums = pltpu.VMEM((ROWS, PAIRS, BLK, LANES), F32)
    weights = pltpu.VMEM((2, 512, 2 * LANES), BF)
    attended = pl.pallas_call(
        kernel,
        out_shape=pltpu.VMEM(x.shape, BF),
        in_specs=[hbm, vmem, hbm, vmem, smem],
        out_specs=vmem,
        scratch_shapes=[
            pltpu.VMEM((PARTS, ROWS, BLK, 512), BF),
            pltpu.VMEM((PARTS, 3 * WIDTH, 512), BF),
            weights, weights, weights,
            blocks, blocks, far_blocks, far_blocks,
            pltpu.VMEM((ROWS, PAIRS, 2 * BLK, LANES), BF),
            sums, sums,
            sub, sub, sub, sub, landed, landed, landed, half_landed, half_landed,
            pltpu.VMEM(x.shape, BF),
            pltpu.VMEM((CHUNKS, GROUPS * CAP, SUB, LANES), BF),
            pltpu.VMEM((CHUNKS - 1, PARTS, ROWS * FAR, SUB, LANES), BF),
            pltpu.VMEM((2, PARTS, ROWS, SUB, LANES), BF),
            pltpu.VMEM((PARTS, ROWS * FAR, SUB, 512), BF),
            pltpu.VMEM((2, PARTS, ROWS, SUB, LANES), BF),
            pltpu.VMEM((2 * 8, LANES), jnp.int32),
            pltpu.VMEM((GROUPS, 1, LANES), jnp.int32),
            pltpu.VMEM((GROUPS, 1, LANES), jnp.int32),
            pltpu.SMEM((GROUPS, 1, LANES), jnp.int32),
            pltpu.VMEM((2 * 8, LANES), jnp.int32),
            pltpu.SMEM((2 * 8, LANES), jnp.int32),
            dma((CHUNKS,)), dma((CHUNKS,)), dma(()), dma(()), dma(()), dma(()),
            dma((8,)), dma((8,)), dma((8,)), dma((8,)),
            dma((CHUNKS + 1,)), dma((CHUNKS + 1,)), dma((CHUNKS + 1,)), dma((CHUNKS,)), dma((PARTS,)),
            dma((2,)),
        ],
        compiler_params=pltpu.CompilerParams(
            collective_id=0, has_side_effects=True, vmem_limit_bytes=57 * 2**20),
        name="block_sparse_layer",
    )(x, gain.reshape(1, 512), w_own, jnp.transpose(targets), sharp)
    return jnp.dot(attended, wf, preferred_element_type=F32).astype(BF)


def solution(mesh):
    placed = (P(("seq", "head"), None), P(), P(), P(None, None, "head"), P(), P("seq", None))
    return jax.shard_map(
        on_device, mesh=mesh, in_specs=placed, out_specs=P(("seq", "head"), None), check_vma=False
    )
```
